256 devices in a mesh: slab: 32 (over z, x), blk: 8 (over y, core).
Axes of the slice: x: 4, y: 4, z: 8, core: 2. Of those that a mesh axis runs over, the one named last changes fastest.
Arguments:
- columns: float32 [65536, 4096], P('slab', 'blk'), may hold values from -40 to 40
- movers: int32 [2, 8], P(None, 'blk'), may hold values 0 or 1
Outputs:
- rotated: float32 [65536, 4096], P('slab', 'blk')
The draws below stay inside these ranges and needn't reach their ends.
All inputs are finite; a program needn't handle non-finite values. No bound on the sum of `movers` on one device may be relied on, other than what follows from the above.
Results may differ from the reference program's by a relative error of at most 0.00016.
Values sent between devices are 32-bit elements; how exact they have to be, the bound alone decides.
No kernel may reach another device: no remote copies, remote signals or barrier semaphores. Data moves between devices by JAX's collectives and lax.ppermute only.
A program may use at most 64 MiB of HBM per device.

```python
import math
import jax
import jax.numpy as jnp
from jax import lax

BLOCK = 256
ROUNDS = 2
NS_STEPS = 12
ROWS = 65536
COLS = 4096
N_BLK = 8


def draw_columns(key, part):
    key = jax.random.fold_in(key, 11)
    key_base, key_cols, key_rows, key_common, key_share, key_load, key_factor = jax.random.split(key, 7)
    col_scale = jnp.exp(jax.random.uniform(key_cols, (COLS,), jnp.float32, math.log(0.5), math.log(5.0)))
    row_scale = jnp.exp(jax.random.uniform(key_rows, (ROWS, 1), jnp.float32, math.log(0.5), math.log(2.0)))
    base = jax.random.normal(key_base, (ROWS, COLS), jnp.float32)
    shared_weight = 0.4
    load_scale = 0.25
    common = jax.random.normal(key_common, (ROWS, 1), jnp.float32)
    share_gain = jax.random.uniform(key_share, (1, COLS), jnp.float32, 0.5, 1.5)
    base = base + shared_weight * common * share_gain
    loadings = load_scale * jax.random.normal(key_load, (8, COLS), jnp.float32)
    factors = jax.random.normal(key_factor, (ROWS, 8), jnp.float32)
    for factor_index in range(8):
        base = base + factors[:, factor_index:factor_index + 1] * loadings[factor_index][None, :]
    return jnp.clip(base * row_scale * col_scale[None, :], -40.0, 40.0)


def with_ends(drawn, own_key, least, high):
    longest = drawn.shape.index(max(drawn.shape))
    spots = []
    for shift in (0, 1):
        where = [jax.random.randint(jax.random.fold_in(own_key, axis), (), 0, length) for axis, length in enumerate(drawn.shape)]
        where[longest] = (where[longest] + shift) % drawn.shape[longest]
        spots.append(tuple(where))
    return drawn.at[spots[0]].set(least).at[spots[1]].set(high)


def setup_inputs(seed: int = 0) -> dict:
    keys = jax.random.split(jax.random.key(seed), 3)
    columns = draw_columns(jax.random.fold_in(keys[2], 71), 0)
    movers = with_ends((jax.random.randint(keys[1], (ROUNDS, N_BLK), 0, 2) < 1).astype(jnp.int32), jax.random.fold_in(keys[1], 1), 0, 1)
    return {"columns": columns, "movers": movers}


epsilon = 1e-06

def skew_rows(gram_rows, col_norms, first_row, half):
    nrows = gram_rows.shape[0]
    width = gram_rows.shape[1]
    row_ids = first_row + jnp.arange(nrows, dtype=jnp.int32)
    col_ids = jnp.arange(width, dtype=jnp.int32)
    mine = lax.dynamic_slice_in_dim(col_norms, first_row, nrows)
    diff = mine[:, None] - col_norms[None, :]
    total = mine[:, None] + col_norms[None, :]
    cross = (row_ids[:, None] < half) != (col_ids[None, :] < half)
    value = -gram_rows * diff / (diff * diff + 0.25 * total * total + epsilon)
    return jnp.where(cross, value, jnp.float32(0.0))

def start_rows(skew_part, first_row, skew_total):
    nrows, width = skew_part.shape
    row_ids = first_row + jnp.arange(nrows, dtype=jnp.int32)
    col_ids = jnp.arange(width, dtype=jnp.int32)
    identity = (row_ids[:, None] == col_ids[None, :]).astype(jnp.float32)
    return (identity + skew_part) / (4.0 * jnp.sqrt(width + skew_total))

def rotation(gram_matrix):
    width = gram_matrix.shape[0]
    col_norms = jnp.diagonal(gram_matrix)
    skew_part = skew_rows(gram_matrix, col_norms, 0, width // 2)
    iterate = start_rows(skew_part, 0, jnp.sum(skew_part * skew_part))

    def newton(step_index, value):
        outer = jnp.dot(value, value.T, precision=lax.Precision.HIGHEST, preferred_element_type=jnp.float32)
        return 1.5 * value - 0.5 * jnp.dot(outer, value, precision=lax.Precision.HIGHEST, preferred_element_type=jnp.float32)
    return lax.fori_loop(0, NS_STEPS, newton, iterate)

def reference(columns, movers):
    current = columns.reshape(ROWS, N_BLK, 2 * BLOCK)
    for round_index in range(ROUNDS):
        gram_all = jnp.einsum('mpi,mpj->pij', current, current, precision=lax.Precision.HIGHEST)
        turns = jax.vmap(rotation)(gram_all)
        rotated_pairs = jnp.einsum('mpi,pij->mpj', current, turns, precision=lax.Precision.HIGHEST)
        first = rotated_pairs[:, :, :BLOCK]
        second = rotated_pairs[:, :, BLOCK:]
        flag = (movers[round_index] == 1)[None, :, None]
        moving = jnp.where(flag, first, second)
        staying = jnp.where(flag, second, first)
        arrived = jnp.roll(moving, 1, axis=1)
        current = jnp.concatenate([staying, arrived], axis=2)
    return current.reshape(ROWS, COLS)
```

```python
import jax
import jax.numpy as jnp
from jax import lax
from jax.experimental import pallas as pl
from jax.experimental.pallas import tpu as pltpu
from jax.sharding import PartitionSpec as P

ROUNDS = 2
HALF = 256
SLABS = 32
CHUNK = 18
VMEM_BYTES = 40 * 2**20
EPS = 1e-6
F32 = jnp.float32
BF16 = jnp.bfloat16
NN = (((1,), (0,)), ((), ()))
NT = (((1,), (1,)), ((), ()))
TN = (((0,), (0,)), ((), ()))


def split(x):
    high = x.astype(BF16)
    low = (x - high.astype(F32)).astype(BF16)
    return high, low


def dot3(left, right, dims):
    def one(a, b):
        return lax.dot_general(a, b, dims, preferred_element_type=F32)
    return one(left[0], right[0]) + (one(left[0], right[1]) + one(left[1], right[0]))


def weight(gap, eye):
    gap_parts = split(gap)
    square = dot3(gap_parts, gap_parts, NN)
    inner = 0.375 * eye + 0.3125 * gap + 0.0625 * square
    return eye + 0.5 * gap + dot3(split(square), split(inner), NN)


def rotation_kernel(flag_ref, packed_ref, stay_ref, move_ref):
    left = [packed_ref[CHUNK * k:CHUNK * k + 8, :] for k in range(SLABS)]
    right = [packed_ref[CHUNK * k + 8:CHUNK * k + 16, :] for k in range(SLABS)]
    cross = jnp.concatenate([jnp.concatenate(left, 0), jnp.concatenate(right, 0)], 1)
    norm_a = jnp.concatenate([packed_ref[16:17, :], packed_ref[17:18, :]], 1)
    norm_m = jnp.concatenate([packed_ref[CHUNK + 16:CHUNK + 17, :], packed_ref[CHUNK + 17:CHUNK + 18, :]], 1)
    rows = lax.broadcasted_iota(jnp.int32, (HALF, HALF), 0)
    cols = lax.broadcasted_iota(jnp.int32, (HALF, HALF), 1)
    eye = (rows == cols).astype(F32)
    norm_a_col = jnp.transpose(jnp.broadcast_to(norm_a, (HALF, HALF)))
    diff = norm_a_col - norm_m
    total = norm_a_col + norm_m
    skew = -cross * diff / (diff * diff + 0.25 * total * total + EPS)
    scale = 1.0 / (4.0 * jnp.sqrt(2.0 * HALF + 2.0 * jnp.sum(skew * skew, keepdims=True)))
    start = scale * skew
    parts = split(start)
    s2 = scale * scale
    w1 = weight(eye - (s2 * eye + dot3(parts, parts, NT)), eye)
    w2 = weight(eye - (s2 * eye + dot3(parts, parts, TN)), eye)
    e1, e2 = scale * w1, scale * w2
    o = dot3(split(w1), parts, NN)

    def two_steps(_, carry):
        e1, e2, o = carry
        e1p, e2p, op = split(e1), split(e2), split(o)
        w1 = split(weight(eye - (dot3(e1p, e1p, NN) + dot3(op, op, NT)), eye))
        w2 = split(weight(eye - (dot3(e2p, e2p, NN) + dot3(op, op, TN)), eye))
        return dot3(w1, e1p, NN), dot3(w2, e2p, NN), dot3(w1, op, NN)

    e1, e2, o = lax.fori_loop(0, 5, two_steps, (e1, e2, o))
    minus_ot = -jnp.transpose(o)

    @pl.when(flag_ref[0] == 1)
    def _():
        move_ref[:HALF, :] = e1
        move_ref[HALF:, :] = minus_ot
        stay_ref[:HALF, :] = o
        stay_ref[HALF:, :] = e2

    @pl.when(flag_ref[0] != 1)
    def _():
        stay_ref[:HALF, :] = e1
        stay_ref[HALF:, :] = minus_ot
        move_ref[:HALF, :] = o
        move_ref[HALF:, :] = e2


def rotation(flag, packed):
    out = jax.ShapeDtypeStruct((2 * HALF, HALF), F32)
    return pl.pallas_call(
        rotation_kernel,
        out_shape=(out, out),
        in_specs=[pl.BlockSpec(memory_space=pltpu.SMEM), pl.BlockSpec(memory_space=pltpu.VMEM)],
        out_specs=[pl.BlockSpec(memory_space=pltpu.VMEM)] * 2,
        compiler_params=pltpu.CompilerParams(vmem_limit_bytes=VMEM_BYTES),
        name="rotation",
    )(flag, packed)


def gram_add(a, m, acc_ref, norm_ref):
    acc_ref[...] += dot3(split(a), split(m), TN)
    norm_ref[0:1, :] += jnp.sum(a * a, axis=0, keepdims=True)
    norm_ref[1:2, :] += jnp.sum(m * m, axis=0, keepdims=True)


def gram_pack(acc_ref, norm_ref, packed_ref):
    packed_ref[...] = jnp.zeros_like(packed_ref)
    for k in range(SLABS):
        packed_ref[CHUNK * k:CHUNK * k + 8, :] = acc_ref[8 * k:8 * k + 8, :128]
        packed_ref[CHUNK * k + 8:CHUNK * k + 16, :] = acc_ref[8 * k:8 * k + 8, 128:]
    for i in range(2):
        packed_ref[CHUNK * i + 16:CHUNK * i + 17, :] = norm_ref[i:i + 1, :128]
        packed_ref[CHUNK * i + 17:CHUNK * i + 18, :] = norm_ref[i:i + 1, 128:]


def gram_kernel(a_ref, m_ref, packed_ref, acc_ref, norm_ref):
    step = pl.program_id(0)

    @pl.when(step == 0)
    def _():
        acc_ref[...] = jnp.zeros_like(acc_ref)
        norm_ref[...] = jnp.zeros_like(norm_ref)

    gram_add(a_ref[...], m_ref[...], acc_ref, norm_ref)

    @pl.when(step == pl.num_programs(0) - 1)
    def _():
        gram_pack(acc_ref, norm_ref, packed_ref)


def gram(a, m, m_block, tile=512):
    return pl.pallas_call(
        gram_kernel,
        grid=(a.shape[0] // tile,),
        out_shape=jax.ShapeDtypeStruct((SLABS * CHUNK, 128), F32),
        in_specs=[
            pl.BlockSpec((tile, HALF), lambda i: (i, 0)),
            pl.BlockSpec((tile, HALF), lambda i: (i, m_block)),
        ],
        out_specs=pl.BlockSpec((SLABS * CHUNK, 128), lambda i: (0, 0)),
        scratch_shapes=[pltpu.VMEM((HALF, HALF), F32), pltpu.VMEM((8, HALF), F32)],
        compiler_params=pltpu.CompilerParams(vmem_limit_bytes=VMEM_BYTES),
        name="gram",
    )(a, m)


def rotate_kernel(a_ref, m_ref, q_ref, out_ref):
    out_ref[...] = dot3(split(a_ref[...]), split(q_ref[:HALF, :]), NN) + dot3(
        split(m_ref[...]), split(q_ref[HALF:, :]), NN
    )


def rotate(a, m, m_block, q, tile=512):
    return pl.pallas_call(
        rotate_kernel,
        grid=(a.shape[0] // tile,),
        out_shape=jax.ShapeDtypeStruct((a.shape[0], HALF), F32),
        in_specs=[
            pl.BlockSpec((tile, HALF), lambda i: (i, 0)),
            pl.BlockSpec((tile, HALF), lambda i: (i, m_block)),
            pl.BlockSpec((2 * HALF, HALF), lambda i: (0, 0)),
        ],
        out_specs=pl.BlockSpec((tile, HALF), lambda i: (i, 0)),
        compiler_params=pltpu.CompilerParams(vmem_limit_bytes=VMEM_BYTES),
        name="rotate",
    )(a, m, q)


def passed_along(value):
    count = lax.axis_size("blk")
    return lax.ppermute(value, "blk", [(source, (source + 1) % count) for source in range(count)])


def summed(packed):
    shares = packed.reshape(SLABS, CHUNK // 2, 2, 128)
    mine = jnp.sum(lax.all_to_all(shares, "slab", 0, 0), axis=0)
    whole = lax.all_to_all(jnp.broadcast_to(mine[None], shares.shape), "slab", 0, 0)
    return whole.reshape(SLABS * CHUNK, 128)


def local(columns, movers):
    a, m, m_block = columns, columns, 1
    for round_index in range(ROUNDS):
        packed = summed(gram(a, m, m_block))
        stay, move = rotation(movers[round_index], packed)
        arrived = passed_along(rotate(a, m, m_block, move))
        a, m, m_block = rotate(a, m, m_block, stay), arrived, 0
    return jnp.concatenate([a, m], axis=1)


def solution(mesh):
    placed = (P("slab", "blk"), P(None, "blk"))
    return jax.shard_map(
        local, mesh=mesh, in_specs=placed, out_specs=P("slab", "blk"), check_vma=False
    )
```

```python
import jax
import jax.numpy as jnp
from jax import lax
from jax.experimental import pallas as pl
from jax.experimental.pallas import tpu as pltpu
from jax.sharding import PartitionSpec as P

HALF = 256
PAIR = 2 * HALF
SLABS = 32
CHUNK = 20
EPS = 1e-6
VMEM_BYTES = 40 * 2**20
F32 = jnp.float32
BF16 = jnp.bfloat16
NN = (((1,), (0,)), ((), ()))
NT = (((1,), (1,)), ((), ()))
TN = (((0,), (0,)), ((), ()))


def split(x):
    high = x.astype(BF16)
    low = (x - high.astype(F32)).astype(BF16)
    return high, low


def dot3(left, right, dims):
    def one(a, b):
        return lax.dot_general(a, b, dims, preferred_element_type=F32)

    return one(left[0], right[0]) + (one(left[0], right[1]) + one(left[1], right[0]))


def call(kernel, name, out_shape, flops, **kwargs):
    return pl.pallas_call(
        kernel,
        out_shape=out_shape,
        compiler_params=pltpu.CompilerParams(vmem_limit_bytes=VMEM_BYTES),
        cost_estimate=pl.CostEstimate(flops=flops, bytes_accessed=2**22, transcendentals=0),
        name=name,
        **kwargs,
    )


def blocks(tile, width, block=0):
    return pl.BlockSpec((tile, width), lambda i: (i, block))


def whole(shape):
    return pl.BlockSpec(shape, lambda i: (0,) * len(shape))


def two_steps(e1, e2, o, eye):
    op, e1p, e2p = split(o), split(e1), split(e2)
    d1 = eye - (dot3(op, op, NT) + dot3(e1p, e1p, NN))
    d2 = eye - (dot3(op, op, TN) + dot3(e2p, e2p, NN))
    w1, w2 = weights(d1, d2, eye)
    w1, w2 = split(w1), split(w2)
    return dot3(w1, e1p, NN), dot3(w2, e2p, NN), dot3(w1, op, NN)


def weights(d1, d2, eye):
    d1p, d2p = split(d1), split(d2)
    q1 = dot3(d1p, d1p, NN)
    q2 = dot3(d2p, d2p, NN)
    i1 = split(0.375 * eye + 0.3125 * d1 + 0.0625 * q1)
    i2 = split(0.375 * eye + 0.3125 * d2 + 0.0625 * q2)
    w1 = eye + 0.5 * d1 + dot3(split(q1), i1, NN)
    w2 = eye + 0.5 * d2 + dot3(split(q2), i2, NN)
    return w1, w2


def rotation_kernel(flag_ref, packed_ref, stay_ref, move_ref):
    left = [packed_ref[CHUNK * k:CHUNK * k + 8, :] for k in range(SLABS)]
    right = [packed_ref[CHUNK * k + 8:CHUNK * k + 16, :] for k in range(SLABS)]
    cross = jnp.concatenate([jnp.concatenate(left, 0), jnp.concatenate(right, 0)], 1)
    norms = packed_ref[16:20, :]
    for k in range(1, SLABS):
        norms = norms + packed_ref[CHUNK * k + 16:CHUNK * k + 20, :]
    norm_a = jnp.concatenate([norms[0:1], norms[1:2]], 1)
    norm_m = jnp.concatenate([norms[2:3], norms[3:4]], 1)
    rows = lax.broadcasted_iota(jnp.int32, (HALF, HALF), 0)
    cols = lax.broadcasted_iota(jnp.int32, (HALF, HALF), 1)
    eye = (rows == cols).astype(F32)
    norm_a = jnp.transpose(jnp.broadcast_to(norm_a, (HALF, HALF)))
    diff = norm_a - norm_m
    total = norm_a + norm_m
    skew = -cross * diff / (diff * diff + 0.25 * total * total + EPS)
    scale = 1.0 / (4.0 * jnp.sqrt(PAIR + 2.0 * jnp.sum(skew * skew, keepdims=True)))
    start = scale * skew
    parts = split(start)
    own = (1.0 - scale * scale) * eye
    w1, w2 = weights(own - dot3(parts, parts, NT), own - dot3(parts, parts, TN), eye)
    e1, e2, o = scale * w1, scale * w2, dot3(split(w1), parts, NN)
    for _ in range(5):
        e1, e2, o = two_steps(e1, e2, o, eye)
    minus_ot = -jnp.transpose(o)

    @pl.when(flag_ref[0] == 1)
    def _():
        move_ref[:HALF, :] = e1
        move_ref[HALF:, :] = minus_ot
        stay_ref[:HALF, :] = o
        stay_ref[HALF:, :] = e2

    @pl.when(flag_ref[0] != 1)
    def _():
        stay_ref[:HALF, :] = e1
        stay_ref[HALF:, :] = minus_ot
        move_ref[:HALF, :] = o
        move_ref[HALF:, :] = e2


def rotation(flag, packed):
    out = jax.ShapeDtypeStruct((PAIR, HALF), F32)
    return call(
        rotation_kernel,
        "rotation",
        (out, out),
        10**10,
        in_specs=[pl.BlockSpec(memory_space=pltpu.SMEM), pl.BlockSpec(memory_space=pltpu.VMEM)],
        out_specs=[pl.BlockSpec(memory_space=pltpu.VMEM)] * 2,
    )(flag, packed)


def inner_kernel(width, a_ref, m_ref, packed_ref, norm_ref, acc_ref):
    step = pl.program_id(0)

    @pl.when(step == 0)
    def _():
        acc_ref[...] = jnp.zeros_like(acc_ref)
        norm_ref[...] = jnp.zeros_like(norm_ref)

    a, m = a_ref[...], m_ref[...]
    acc_ref[...] += dot3(split(a), split(m), TN)
    norm_ref[0:1, :] += jnp.sum(a * a, axis=0, keepdims=True)
    if width == HALF:
        norm_ref[1:2, :] += jnp.sum(m * m, axis=0, keepdims=True)

    @pl.when(step == pl.num_programs(0) - 1)
    def _():
        per = 8 * width // 128
        for k in range(SLABS):
            for b in range(width // 128):
                packed_ref[per * k + 8 * b:per * k + 8 * b + 8, :] = acc_ref[8 * k:8 * k + 8, 128 * b:128 * b + 128]


def inner(a, m, width, block, tile=512):
    rows = HALF * width // 128
    return call(
        lambda *refs: inner_kernel(width, *refs),
        "inner",
        (jax.ShapeDtypeStruct((rows, 128), F32), jax.ShapeDtypeStruct((8, HALF), F32)),
        6 * a.shape[0] * HALF * width,
        grid=(a.shape[0] // tile,),
        in_specs=[blocks(tile, HALF), blocks(tile, width, block)],
        out_specs=[whole((rows, 128)), whole((8, HALF))],
        scratch_shapes=[pltpu.VMEM((HALF, width), F32)],
    )(a, m)


def fill(out_ref, cross, norm_a, norm_m):
    chunk = jnp.concatenate(
        [cross[:, :128], cross[:, 128:], norm_a[:, :128], norm_a[:, 128:], norm_m[:, :128], norm_m[:, 128:]], 0
    )
    for k in range(SLABS):
        out_ref[CHUNK * k:CHUNK * k + CHUNK, :] = chunk


def share_kernel(parts_ref, norm_ref, out_ref):
    total = parts_ref[0:16, :]
    for k in range(1, SLABS):
        total = total + parts_ref[16 * k:16 * k + 16, :]
    cross = jnp.concatenate([total[:8], total[8:]], 1)
    fill(out_ref, cross, norm_ref[0:1, :], norm_ref[1:2, :])


def project_kernel(parts_ref, move_ref, norm_a_ref, norm_m_ref, out_ref):
    total = parts_ref[0:32, :]
    for k in range(1, SLABS):
        total = total + parts_ref[32 * k:32 * k + 32, :]
    wide = jnp.concatenate([total[8 * b:8 * b + 8] for b in range(4)], 1)
    wide = jnp.concatenate([wide, wide], 0)
    cross = dot3(split(wide), split(move_ref[...]), NN)[:8]
    fill(out_ref, cross, norm_a_ref[0:1, :], norm_m_ref[0:1, :])


def payload(kernel, *arrays):
    return call(kernel, "payload", jax.ShapeDtypeStruct((SLABS * CHUNK, 128), F32), 10**7)(*arrays)


def turn_kernel(a_ref, q_ref, out_ref, norm_ref):
    @pl.when(pl.program_id(0) == 0)
    def _():
        norm_ref[...] = jnp.zeros_like(norm_ref)

    out = dot3(split(a_ref[...]), split(q_ref[...]), NN)
    out_ref[...] = out
    norm_ref[0:1, :] += jnp.sum(out * out, axis=0, keepdims=True)


def turn(a, q, tile=512):
    rows = a.shape[0]
    return call(
        turn_kernel,
        "turn",
        (jax.ShapeDtypeStruct((rows, HALF), F32), jax.ShapeDtypeStruct((8, HALF), F32)),
        6 * rows * PAIR * HALF,
        grid=(rows // tile,),
        in_specs=[blocks(tile, PAIR), whole(q.shape)],
        out_specs=[blocks(tile, HALF), whole((8, HALF))],
    )(a, q)


def last_kernel(a_ref, m_ref, q_ref, *refs):
    refs[-1][...] = dot3(split(a_ref[...]), split(q_ref[:HALF, :]), NN) + dot3(
        split(m_ref[...]), split(q_ref[HALF:, :]), NN
    )


def last(a, m, q, block, onto=None, tile=512):
    rows = a.shape[0]
    specs = [blocks(tile, HALF), blocks(tile, HALF), whole(q.shape)]
    extra = () if onto is None else (onto,)
    return call(
        last_kernel,
        "last",
        jax.ShapeDtypeStruct((rows, PAIR), F32),
        6 * rows * PAIR * HALF,
        grid=(rows // tile,),
        in_specs=specs + [pl.BlockSpec(memory_space=pl.ANY)] * len(extra),
        out_specs=blocks(tile, HALF, block),
        input_output_aliases={3: 0} if extra else {},
    )(a, m, q, *extra)


def passed_along(value):
    count = lax.axis_size("blk")
    return lax.ppermute(value, "blk", [(source, (source + 1) % count) for source in range(count)])


def exchanged(packed, shape):
    return lax.all_to_all(packed.reshape(SLABS, *shape), "slab", 0, 0).reshape(packed.shape)


def local(columns, movers):
    left_columns = passed_along(columns)

    cross, norms = inner(columns, columns, HALF, 1)
    parts = exchanged(cross, (16, 128))
    packed = exchanged(payload(share_kernel, parts, norms), (CHUNK // 2, 2, 128))
    stay, move = rotation(movers[0], packed)

    left_turn = passed_along(jnp.concatenate([move, stay], axis=0))
    left_move, left_stay = left_turn[:PAIR], left_turn[PAIR:]
    a, _ = turn(columns, stay)
    cross, norm_a = inner(a, left_columns, PAIR, 0)
    parts = exchanged(cross, (32, 128))
    m, norm_m = turn(left_columns, left_move)
    left_m = passed_along(m)
    packed = exchanged(payload(project_kernel, parts, left_move, norm_a, norm_m), (CHUNK // 2, 2, 128))
    stay, move = rotation(movers[1], packed)

    left_move = passed_along(move)
    left_a, _ = turn(left_columns, left_stay)
    out = last(a, m, stay, 0)
    return last(left_a, left_m, left_move, 1, out)


def solution(mesh):
    placed = (P("slab", "blk"), P(None, "blk"))
    return jax.shard_map(
        local, mesh=mesh, in_specs=placed, out_specs=P("slab", "blk"), check_vma=False
    )
```

```python
import jax
import jax.numpy as jnp
from jax import lax
from jax.experimental import pallas as pl
from jax.experimental.pallas import tpu as pltpu
from jax.sharding import PartitionSpec as P

HALF = 256
PAIR = 2 * HALF
SLABS = 32
CHUNK = 20
EPS = 1e-6
VMEM_BYTES = 20 * 2**20
F32 = jnp.float32
BF16 = jnp.bfloat16
NN = (((1,), (0,)), ((), ()))
NT = (((1,), (1,)), ((), ()))
TN = (((0,), (0,)), ((), ()))


def split(x):
    high = x.astype(BF16)
    low = (x - high.astype(F32)).astype(BF16)
    return high, low


def dot3(left, right, dims):
    def one(a, b):
        return lax.dot_general(a, b, dims, preferred_element_type=F32)

    return one(left[0], right[0]) + (one(left[0], right[1]) + one(left[1], right[0]))


def square3(parts):
    high, low = parts
    mixed = lax.dot_general(high, low, NN, preferred_element_type=F32)
    return lax.dot_general(high, high, NN, preferred_element_type=F32) + (mixed + jnp.transpose(mixed))


def call(kernel, name, out_shape, flops, **kwargs):
    return pl.pallas_call(
        kernel,
        out_shape=out_shape,
        compiler_params=pltpu.CompilerParams(vmem_limit_bytes=VMEM_BYTES),
        cost_estimate=pl.CostEstimate(flops=flops, bytes_accessed=2**22, transcendentals=0),
        name=name,
        **kwargs,
    )


VMEM = pl.BlockSpec(memory_space=pltpu.VMEM)
HBM = pl.BlockSpec(memory_space=pltpu.HBM)


def two_steps(e1, e2, o, eye):
    op, e1p, e2p = split(o), split(e1), split(e2)
    d1 = (eye - square3(e1p)) - dot3(op, op, NT)
    d2 = (eye - square3(e2p)) - dot3(op, op, TN)
    w1, w2 = weights(d1, d2, eye)
    w1, w2 = split(w1), split(w2)
    o = dot3(w1, op, NN)
    return dot3(w1, e1p, NN), dot3(w2, e2p, NN), o


def weights(d1, d2, eye):
    d1p, d2p = split(d1), split(d2)
    q1 = square3(d1p)
    q2 = square3(d2p)
    i1 = split(0.375 * eye + 0.3125 * d1 + 0.0625 * q1)
    i2 = split(0.375 * eye + 0.3125 * d2 + 0.0625 * q2)
    w1 = eye + 0.5 * d1 + dot3(split(q1), i1, NN)
    w2 = eye + 0.5 * d2 + dot3(split(q2), i2, NN)
    return w1, w2


def rotation_kernel(flag_ref, packed_ref, *outs):
    move_ref, stay_ref = outs if len(outs) == 2 else (outs[0].at[:PAIR], outs[0].at[PAIR:])
    left = [packed_ref[CHUNK * k:CHUNK * k + 8, :] for k in range(SLABS)]
    right = [packed_ref[CHUNK * k + 8:CHUNK * k + 16, :] for k in range(SLABS)]
    cross = jnp.concatenate([jnp.concatenate(left, 0), jnp.concatenate(right, 0)], 1)
    norms = packed_ref[16:20, :]
    for k in range(1, SLABS):
        norms = norms + packed_ref[CHUNK * k + 16:CHUNK * k + 20, :]
    norm_a = jnp.concatenate([norms[0:1], norms[1:2]], 1)
    norm_m = jnp.concatenate([norms[2:3], norms[3:4]], 1)
    rows = lax.broadcasted_iota(jnp.int32, (HALF, HALF), 0)
    cols = lax.broadcasted_iota(jnp.int32, (HALF, HALF), 1)
    eye = (rows == cols).astype(F32)
    norm_a = jnp.transpose(jnp.broadcast_to(norm_a, (HALF, HALF)))
    diff = norm_a - norm_m
    total = norm_a + norm_m
    skew = -cross * diff / (diff * diff + 0.25 * total * total + EPS)
    scale = 1.0 / (4.0 * jnp.sqrt(PAIR + 2.0 * jnp.sum(skew * skew, keepdims=True)))
    start = scale * skew
    parts = split(start)
    own = (1.0 - scale * scale) * eye
    w1, w2 = weights(own - dot3(parts, parts, NT), own - dot3(parts, parts, TN), eye)
    e1, e2, o = scale * w1, scale * w2, dot3(split(w1), parts, NN)
    for _ in range(5):
        e1, e2, o = two_steps(e1, e2, o, eye)
    minus_ot = -jnp.transpose(o)

    @pl.when(flag_ref[0] == 1)
    def _():
        move_ref[:HALF, :] = e1
        move_ref[HALF:, :] = minus_ot
        stay_ref[:HALF, :] = o
        stay_ref[HALF:, :] = e2

    @pl.when(flag_ref[0] != 1)
    def _():
        stay_ref[:HALF, :] = e1
        stay_ref[HALF:, :] = minus_ot
        move_ref[:HALF, :] = o
        move_ref[HALF:, :] = e2


def rotation(flag, packed, rows):
    return call(
        rotation_kernel,
        "rotation",
        [jax.ShapeDtypeStruct((n, HALF), F32) for n in rows],
        10**10,
        in_specs=[pl.BlockSpec(memory_space=pltpu.SMEM), VMEM],
        out_specs=[VMEM] * len(rows),
    )(flag, packed)


def pack(packed_ref, value):
    width = value.shape[1]
    per = 8 * width // 128
    for k in range(SLABS):
        for b in range(width // 128):
            packed_ref[per * k + 8 * b:per * k + 8 * b + 8, :] = value[8 * k:8 * k + 8, 128 * b:128 * b + 128]


def row_tiles(ref, tile):
    return [pl.ds(start, tile) for start in range(0, ref.shape[0], tile)]


def squares(x):
    return jnp.sum(x.reshape(-1, 8, x.shape[1]) ** 2, axis=0)


def first_kernel(x_ref, packed_ref, norm_ref):
    total, norm = 0.0, 0.0
    for rows in row_tiles(x_ref, 256):
        x = x_ref[rows, :]
        total += dot3(split(x[:, :HALF]), split(x[:, HALF:]), TN)
        norm += squares(x)
    pack(packed_ref, total)
    norm_ref[...] = jnp.concatenate([norm[:, :HALF], norm[:, HALF:]], 0)


def first_inner(x):
    return call(
        first_kernel,
        "first_inner",
        (jax.ShapeDtypeStruct((HALF * HALF // 128, 128), F32), jax.ShapeDtypeStruct((16, HALF), F32)),
        6 * x.shape[0] * HALF * HALF,
        in_specs=[VMEM],
        out_specs=[VMEM] * 2,
    )(x)


def meet_kernel(x_ref, q_ref, left_ref, a_ref, norm_ref, packed_ref, held_ref, sem):
    copy = pltpu.make_async_copy(left_ref, held_ref, sem)
    copy.start()
    q = split(q_ref[PAIR:, :])
    norm, total = 0.0, 0.0
    for rows in row_tiles(x_ref, 512):
        a = dot3(split(x_ref[rows, :]), q, NN)
        a_ref[rows, :] = a
        norm += squares(a)
    norm_ref[...] = norm
    copy.wait()
    for rows in row_tiles(x_ref, 512):
        total += dot3(split(a_ref[rows, :]), split(held_ref[rows, :]), TN)
    pack(packed_ref, total)


def meet(x, q, left):
    rows = x.shape[0]
    return call(
        meet_kernel,
        "meet",
        (
            jax.ShapeDtypeStruct((rows, HALF), F32),
            jax.ShapeDtypeStruct((8, HALF), F32),
            jax.ShapeDtypeStruct((HALF * PAIR // 128, 128), F32),
        ),
        12 * rows * PAIR * HALF,
        in_specs=[VMEM, VMEM, HBM],
        out_specs=[VMEM] * 3,
        scratch_shapes=[pltpu.VMEM((rows, PAIR), F32), pltpu.SemaphoreType.DMA],
    )(x, q, left)


def fill(out_ref, cross, norm_a, norm_m):
    norm_a = jnp.sum(norm_a, axis=0, keepdims=True)
    norm_m = jnp.sum(norm_m, axis=0, keepdims=True)
    chunk = jnp.concatenate(
        [cross[:, :128], cross[:, 128:], norm_a[:, :128], norm_a[:, 128:], norm_m[:, :128], norm_m[:, 128:]], 0
    )
    for k in range(SLABS):
        out_ref[CHUNK * k:CHUNK * k + CHUNK, :] = chunk


def share_kernel(parts_ref, norm_ref, out_ref):
    total = parts_ref[0:16, :]
    for k in range(1, SLABS):
        total = total + parts_ref[16 * k:16 * k + 16, :]
    cross = jnp.concatenate([total[:8], total[8:]], 1)
    fill(out_ref, cross, norm_ref[:8, :], norm_ref[8:, :])


def project_kernel(parts_ref, high_ref, low_ref, norm_a_ref, norm_m_ref, out_ref):
    total = parts_ref[0:32, :]
    for k in range(1, SLABS):
        total = total + parts_ref[32 * k:32 * k + 32, :]
    wide = jnp.concatenate([total[8 * b:8 * b + 8] for b in range(4)], 1)
    wide = jnp.concatenate([wide, wide], 0)
    cross = dot3(split(wide), (high_ref[...], low_ref[...]), NN)[:8]
    fill(out_ref, cross, norm_a_ref[...], norm_m_ref[...])


def payload(kernel, *arrays):
    out = jax.ShapeDtypeStruct((SLABS * CHUNK, 128), F32)
    return call(kernel, "payload", out, 10**7, in_specs=[VMEM] * len(arrays), out_specs=VMEM)(*arrays)


def turn_kernel(first, x_ref, q_ref, out_ref, *refs):
    held_ref, sem = refs[-2:]
    copy = pltpu.make_async_copy(x_ref, held_ref, sem)
    copy.start()
    q = split(q_ref[first:first + PAIR, :])
    copy.wait()
    norm = 0.0
    for rows in row_tiles(held_ref, 512):
        out = dot3(split(held_ref[rows, :]), q, NN)
        out_ref[rows, :] = out
        norm += squares(out)
    if len(refs) > 2:
        norm_ref, high_ref, low_ref = refs[:3]
        norm_ref[...] = norm
        high_ref[...], low_ref[...] = q


def turn(x, q, first, more):
    rows = x.shape[0]
    extra = (
        jax.ShapeDtypeStruct((8, HALF), F32),
        jax.ShapeDtypeStruct((PAIR, HALF), BF16),
        jax.ShapeDtypeStruct((PAIR, HALF), BF16),
    )
    out = (jax.ShapeDtypeStruct((rows, HALF), F32),) + (extra if more else ())
    return call(
        lambda *refs: turn_kernel(first, *refs),
        "turn",
        out,
        6 * rows * PAIR * HALF,
        in_specs=[HBM, VMEM],
        out_specs=(VMEM,) * len(out),
        scratch_shapes=[pltpu.VMEM((rows, PAIR), F32), pltpu.SemaphoreType.DMA],
    )(x, q)


def last_kernel(block, a_ref, m_ref, q_ref, *refs):
    out_ref, came_ref, held_ref, in_sem, out_sems = refs[-5:]
    copy = pltpu.make_async_copy(m_ref, came_ref, in_sem)
    copy.start()
    qa, qm = split(q_ref[:HALF, :]), split(q_ref[HALF:, :])
    for rows in row_tiles(a_ref, 512):
        held_ref[rows, :] = dot3(split(a_ref[rows, :]), qa, NN)
    copy.wait()
    outs = []
    for i, rows in enumerate(row_tiles(a_ref, 512)):
        held_ref[rows, :] += dot3(split(came_ref[rows, :]), qm, NN)
        there = out_ref.at[rows, pl.ds(HALF * block, HALF)]
        outs.append(pltpu.make_async_copy(held_ref.at[rows], there, out_sems.at[i]))
        outs[-1].start()
    for copy in outs:
        copy.wait()


def last(a, m, q, block, onto=None):
    rows = a.shape[0]
    extra = () if onto is None else (onto,)
    held = pltpu.VMEM((rows, HALF), F32)
    return call(
        lambda *refs: last_kernel(block, *refs),
        "last",
        jax.ShapeDtypeStruct((rows, PAIR), F32),
        6 * rows * PAIR * HALF,
        in_specs=[VMEM, HBM, VMEM] + [HBM] * len(extra),
        out_specs=HBM,
        scratch_shapes=[held, held, pltpu.SemaphoreType.DMA, pltpu.SemaphoreType.DMA((rows // 512,))],
        input_output_aliases={3: 0} if extra else {},
    )(a, m, q, *extra)


def passed_along(value):
    count = lax.axis_size("blk")
    return lax.ppermute(value, "blk", [(source, (source + 1) % count) for source in range(count)])


def exchanged(packed, shape):
    return lax.all_to_all(packed.reshape(SLABS, *shape), "slab", 0, 0).reshape(packed.shape)


def local(columns, movers):
    left_columns = passed_along(columns)

    cross, norms = first_inner(columns)
    parts = exchanged(cross, (16, 128))
    packed = exchanged(payload(share_kernel, parts, norms), (CHUNK // 2, 2, 128))
    (both,) = rotation(movers[0], packed, (2 * PAIR,))

    left_both = passed_along(both)
    a, norm_a, cross = meet(columns, both, left_columns)
    parts = exchanged(cross, (32, 128))
    m, norm_m, high, low = turn(left_columns, left_both, 0, True)
    left_m = passed_along(m)
    packed = exchanged(payload(project_kernel, parts, high, low, norm_a, norm_m), (CHUNK // 2, 2, 128))
    move, stay = rotation(movers[1], packed, (PAIR, PAIR))

    left_move = passed_along(move)
    (left_a,) = turn(left_columns, left_both, PAIR, False)
    out = last(a, m, stay, 0)
    return last(left_a, left_m, left_move, 1, out)


def solution(mesh):
    placed = (P("slab", "blk"), P(None, "blk"))
    return jax.shard_map(
        local, mesh=mesh, in_specs=placed, out_specs=P("slab", "blk"), check_vma=False
    )
```

```python
import jax
import jax.numpy as jnp
from jax import lax
from jax.experimental import pallas as pl
from jax.experimental.pallas import tpu as pltpu
from jax.sharding import PartitionSpec as P

HALF = 256
PAIR = 2 * HALF
SLABS = 32
CHUNK = 20
EPS = 1e-6
VMEM_BYTES = 24 * 2**20
F32 = jnp.float32
BF16 = jnp.bfloat16
NN = (((1,), (0,)), ((), ()))
NT = (((1,), (1,)), ((), ()))
TN = (((0,), (0,)), ((), ()))


def split(x):
    high = x.astype(BF16)
    low = (x - high.astype(F32)).astype(BF16)
    return high, low


def dot3(left, right, dims):
    def one(a, b):
        return lax.dot_general(a, b, dims, preferred_element_type=F32)

    return one(left[0], right[0]) + (one(left[0], right[1]) + one(left[1], right[0]))


def square3(parts):
    high, low = parts
    mixed = lax.dot_general(high, low, NN, preferred_element_type=F32)
    return lax.dot_general(high, high, NN, preferred_element_type=F32) + (mixed + jnp.transpose(mixed))


def call(kernel, name, out_shape, flops, **kwargs):
    return pl.pallas_call(
        kernel,
        out_shape=out_shape,
        compiler_params=pltpu.CompilerParams(vmem_limit_bytes=VMEM_BYTES),
        cost_estimate=pl.CostEstimate(flops=flops, bytes_accessed=2**22, transcendentals=0),
        name=name,
        **kwargs,
    )


VMEM = pl.BlockSpec(memory_space=pltpu.VMEM)
HBM = pl.BlockSpec(memory_space=pltpu.HBM)


def in_hbm(x):
    return pltpu.with_memory_space_constraint(x, pltpu.HBM)


def in_vmem(x):
    return pltpu.with_memory_space_constraint(x, pltpu.VMEM)


def row_tiles(ref, tile):
    return [pl.ds(start, tile) for start in range(0, ref.shape[0], tile)]


def two_steps(e1, e2, o, eye):
    op, e1p, e2p = split(o), split(e1), split(e2)
    d1 = (eye - square3(e1p)) - dot3(op, op, NT)
    d2 = (eye - square3(e2p)) - dot3(op, op, TN)
    w1, w2 = weights(d1, d2, eye)
    w1, w2 = split(w1), split(w2)
    o = dot3(w1, op, NN)
    return dot3(w1, e1p, NN), dot3(w2, e2p, NN), o


def weights(d1, d2, eye):
    d1p, d2p = split(d1), split(d2)
    q1 = square3(d1p)
    q2 = square3(d2p)
    i1 = split(0.375 * eye + 0.3125 * d1 + 0.0625 * q1)
    i2 = split(0.375 * eye + 0.3125 * d2 + 0.0625 * q2)
    w1 = eye + 0.5 * d1 + dot3(split(q1), i1, NN)
    w2 = eye + 0.5 * d2 + dot3(split(q2), i2, NN)
    return w1, w2


def rotation_kernel(index, movers_ref, packed_ref, move_ref, stay_ref):
    left = [packed_ref[CHUNK * k:CHUNK * k + 8, :] for k in range(SLABS)]
    right = [packed_ref[CHUNK * k + 8:CHUNK * k + 16, :] for k in range(SLABS)]
    cross = jnp.concatenate([jnp.concatenate(left, 0), jnp.concatenate(right, 0)], 1)
    norms = packed_ref[16:20, :]
    for k in range(1, SLABS):
        norms = norms + packed_ref[CHUNK * k + 16:CHUNK * k + 20, :]
    norm_a = jnp.concatenate([norms[0:1], norms[1:2]], 1)
    norm_m = jnp.concatenate([norms[2:3], norms[3:4]], 1)
    rows = lax.broadcasted_iota(jnp.int32, (HALF, HALF), 0)
    cols = lax.broadcasted_iota(jnp.int32, (HALF, HALF), 1)
    eye = (rows == cols).astype(F32)
    norm_a = jnp.transpose(jnp.broadcast_to(norm_a, (HALF, HALF)))
    diff = norm_a - norm_m
    total = norm_a + norm_m
    skew = -cross * diff / (diff * diff + 0.25 * total * total + EPS)
    scale = 1.0 / (4.0 * jnp.sqrt(PAIR + 2.0 * jnp.sum(skew * skew, keepdims=True)))
    start = scale * skew
    parts = split(start)
    own = (1.0 - scale * scale) * eye
    w1, w2 = weights(own - dot3(parts, parts, NT), own - dot3(parts, parts, TN), eye)
    e1, e2, o = scale * w1, scale * w2, dot3(split(w1), parts, NN)
    for _ in range(5):
        e1, e2, o = two_steps(e1, e2, o, eye)
    minus_ot = -jnp.transpose(o)

    @pl.when(movers_ref[index] == 1)
    def _():
        move_ref[:HALF, :] = e1
        move_ref[HALF:PAIR, :] = minus_ot
        stay_ref[:HALF, :] = o
        stay_ref[HALF:, :] = e2

    @pl.when(movers_ref[index] != 1)
    def _():
        stay_ref[:HALF, :] = e1
        stay_ref[HALF:, :] = minus_ot
        move_ref[:HALF, :] = o
        move_ref[HALF:PAIR, :] = e2

    if move_ref.shape[0] > PAIR:
        move_ref[PAIR:, :] = stay_ref[...]


def rotation(index, movers, packed, rows=PAIR):
    sizes = (rows, PAIR)
    return call(
        lambda *refs: rotation_kernel(index, *refs),
        "rotation",
        [jax.ShapeDtypeStruct((n, HALF), F32) for n in sizes],
        10**10,
        in_specs=[pl.BlockSpec(memory_space=pltpu.SMEM), VMEM],
        out_specs=[VMEM] * 2,
    )(movers, packed)


def pack(packed_ref, value):
    width = value.shape[1]
    per = 8 * width // 128
    for k in range(SLABS):
        for b in range(width // 128):
            packed_ref[per * k + 8 * b:per * k + 8 * b + 8, :] = value[8 * k:8 * k + 8, 128 * b:128 * b + 128]


def squares(x):
    return jnp.sum(x.reshape(-1, 8, x.shape[1]) ** 2, axis=0)


def first_kernel(x_ref, packed_ref, norm_ref):
    total, norm = 0.0, 0.0
    for rows in row_tiles(x_ref, 256):
        x = x_ref[rows, :]
        total += dot3(split(x[:, :HALF]), split(x[:, HALF:]), TN)
        norm += squares(x)
    pack(packed_ref, total)
    norm_ref[...] = jnp.concatenate([norm[:, :HALF], norm[:, HALF:]], 0)


def first_inner(x):
    return call(
        first_kernel,
        "first_inner",
        (jax.ShapeDtypeStruct((HALF * HALF // 128, 128), F32), jax.ShapeDtypeStruct((16, HALF), F32)),
        6 * x.shape[0] * HALF * HALF,
        in_specs=[VMEM],
        out_specs=[VMEM] * 2,
    )(in_vmem(x))


def meet_kernel(x_ref, q_ref, left_ref, a_ref, norm_ref, packed_ref):
    q = split(q_ref[...])
    norm, total = 0.0, 0.0
    for rows in row_tiles(x_ref, 512):
        a = dot3(split(x_ref[rows, :]), q, NN)
        a_ref[rows, :] = a
        norm += squares(a)
    norm_ref[...] = norm
    for rows in row_tiles(x_ref, 512):
        total += dot3(split(a_ref[rows, :]), split(left_ref[rows, :]), TN)
    pack(packed_ref, total)


def meet(x, q, left):
    rows = x.shape[0]
    return call(
        meet_kernel,
        "meet",
        (
            jax.ShapeDtypeStruct((rows, HALF), F32),
            jax.ShapeDtypeStruct((8, HALF), F32),
            jax.ShapeDtypeStruct((HALF * PAIR // 128, 128), F32),
        ),
        12 * rows * PAIR * HALF,
        in_specs=[VMEM] * 3,
        out_specs=[VMEM] * 3,
    )(in_vmem(x), q, in_vmem(left))


def fill(out_ref, cross, norm_a, norm_m):
    norm_a = jnp.sum(norm_a, axis=0, keepdims=True)
    norm_m = jnp.sum(norm_m, axis=0, keepdims=True)
    chunk = jnp.concatenate(
        [cross[:, :128], cross[:, 128:], norm_a[:, :128], norm_a[:, 128:], norm_m[:, :128], norm_m[:, 128:]], 0
    )
    for k in range(SLABS):
        out_ref[CHUNK * k:CHUNK * k + CHUNK, :] = chunk


def share_kernel(parts_ref, norm_ref, out_ref):
    total = parts_ref[0:16, :]
    for k in range(1, SLABS):
        total = total + parts_ref[16 * k:16 * k + 16, :]
    cross = jnp.concatenate([total[:8], total[8:]], 1)
    fill(out_ref, cross, norm_ref[:8, :], norm_ref[8:, :])


def project_kernel(parts_ref, high_ref, low_ref, norm_a_ref, norm_m_ref, out_ref):
    total = parts_ref[0:32, :]
    for k in range(1, SLABS):
        total = total + parts_ref[32 * k:32 * k + 32, :]
    wide = jnp.concatenate([total[8 * b:8 * b + 8] for b in range(4)], 1)
    wide = jnp.concatenate([wide, wide], 0)
    cross = dot3(split(wide), (high_ref[...], low_ref[...]), NN)[:8]
    fill(out_ref, cross, norm_a_ref[...], norm_m_ref[...])


def payload(kernel, *arrays):
    out = jax.ShapeDtypeStruct((SLABS * CHUNK, 128), F32)
    return call(kernel, "payload", out, 10**7, in_specs=[VMEM] * len(arrays), out_specs=VMEM)(*arrays)


def turn_kernel(x_ref, q_ref, out_ref, norm_ref, high_ref, low_ref, held_ref, turn_ref, out_sems):
    pltpu.sync_copy(q_ref.at[pl.ds(0, PAIR)], turn_ref)
    q = split(turn_ref[...])
    high_ref[...], low_ref[...] = q
    norm, outs = 0.0, []
    for i, rows in enumerate(row_tiles(x_ref, 512)):
        out = dot3(split(x_ref[rows, :]), q, NN)
        held_ref[rows, :] = out
        norm += squares(out)
        outs.append(pltpu.make_async_copy(held_ref.at[rows], out_ref.at[rows], out_sems.at[i]))
        outs[-1].start()
    norm_ref[...] = norm
    for copy in outs:
        copy.wait()


def turn(x, q):
    rows = x.shape[0]
    return call(
        turn_kernel,
        "turn",
        (
            pltpu.HBM((rows, HALF), F32),
            jax.ShapeDtypeStruct((8, HALF), F32),
            jax.ShapeDtypeStruct((PAIR, HALF), BF16),
            jax.ShapeDtypeStruct((PAIR, HALF), BF16),
        ),
        30 * 10**9,
        in_specs=[VMEM, HBM],
        out_specs=[HBM] + [VMEM] * 3,
        scratch_shapes=[
            pltpu.VMEM((rows, HALF), F32),
            pltpu.VMEM((PAIR, HALF), F32),
            pltpu.SemaphoreType.DMA((rows // 512,)),
        ],
    )(in_vmem(x), in_hbm(q))


def ready_kernel(x_ref, m_ref, q_ref, high_ref, low_ref):
    q = split(q_ref[PAIR:, :])
    for rows in row_tiles(x_ref, 512):
        high_ref[rows, HALF:], low_ref[rows, HALF:] = split(m_ref[rows, :])
        out = dot3(split(x_ref[rows, :]), q, NN)
        high_ref[rows, :HALF], low_ref[rows, :HALF] = split(out)


def ready(x, m, q):
    rows = x.shape[0]
    out = jax.ShapeDtypeStruct((rows, PAIR), BF16)
    return call(
        ready_kernel,
        "ready",
        (out, out),
        6 * rows * PAIR * HALF,
        in_specs=[VMEM] * 3,
        out_specs=[VMEM] * 2,
    )(in_vmem(x), in_vmem(m), in_vmem(q))


def right_kernel(high_ref, low_ref, q_ref, onto_ref, out_ref, held_ref, sems):
    q = split(q_ref[...])
    outs = []
    for i, rows in enumerate(row_tiles(high_ref, 512)):
        held_ref[rows, :] = dot3((high_ref[rows, :], low_ref[rows, :]), q, NN)
        outs.append(pltpu.make_async_copy(held_ref.at[rows], out_ref.at[rows, pl.ds(HALF, HALF)], sems.at[i]))
        outs[-1].start()
    for copy in outs:
        copy.wait()


def right(high, low, q, onto):
    rows = high.shape[0]
    return call(
        right_kernel,
        "right",
        jax.ShapeDtypeStruct((rows, PAIR), F32),
        6 * rows * PAIR * HALF,
        in_specs=[VMEM, VMEM, VMEM, HBM],
        out_specs=HBM,
        scratch_shapes=[pltpu.VMEM((rows, HALF), F32), pltpu.SemaphoreType.DMA((rows // 512,))],
        input_output_aliases={3: 0},
    )(high, low, q, onto)


def left_kernel(a_ref, m_ref, q_ref, out_ref, held_ref, sems):
    qa, qm = split(q_ref[:HALF, :]), split(q_ref[HALF:, :])
    outs = []
    for i, rows in enumerate(row_tiles(a_ref, 512)):
        held_ref[rows, :] = dot3(split(a_ref[rows, :]), qa, NN) + dot3(split(m_ref[rows, :]), qm, NN)
        outs.append(pltpu.make_async_copy(held_ref.at[rows], out_ref.at[rows, pl.ds(0, HALF)], sems.at[i]))
        outs[-1].start()
    for copy in outs:
        copy.wait()


def left(a, m, q):
    rows = a.shape[0]
    return call(
        left_kernel,
        "left",
        jax.ShapeDtypeStruct((rows, PAIR), F32),
        6 * rows * PAIR * HALF,
        in_specs=[VMEM] * 3,
        out_specs=HBM,
        scratch_shapes=[pltpu.VMEM((rows, HALF), F32), pltpu.SemaphoreType.DMA((rows // 512,))],
    )(a, in_vmem(m), q)


def passed_along(value):
    count = lax.axis_size("blk")
    return lax.ppermute(value, "blk", [(source, (source + 1) % count) for source in range(count)])


def exchanged(packed, shape):
    return lax.all_to_all(packed.reshape(SLABS, *shape), "slab", 0, 0).reshape(packed.shape)


def local(columns, movers):
    left_columns = passed_along(columns)

    cross, norms = first_inner(columns)
    movers, cross = lax.optimization_barrier((movers[:, 0], cross))
    parts = exchanged(cross, (16, 128))
    packed = exchanged(payload(share_kernel, parts, norms), (CHUNK // 2, 2, 128))
    both, stay = rotation(0, movers, packed, 2 * PAIR)

    left_both = passed_along(both)
    a, norm_a, cross = meet(columns, stay, left_columns)
    parts = exchanged(cross, (32, 128))
    m, norm_m, high, low = turn(left_columns, left_both)
    left_m = passed_along(m)
    packed = exchanged(payload(project_kernel, parts, high, low, norm_a, norm_m), (CHUNK // 2, 2, 128))
    move, stay = rotation(1, movers, packed)

    left_move = passed_along(move)
    left_high, left_low = ready(left_columns, left_m, left_both)
    out = left(a, m, stay)
    return right(left_high, left_low, left_move, out)


def solution(mesh):
    placed = (P("slab", "blk"), P(None, "blk"))
    return jax.shard_map(
        local, mesh=mesh, in_specs=placed, out_specs=P("slab", "blk"), check_vma=False
    )
```

```python
import jax
import jax.numpy as jnp
from jax import lax
from jax.experimental import pallas as pl
from jax.experimental.pallas import tpu as pltpu
from jax.sharding import PartitionSpec as P

HALF = 256
PAIR = 2 * HALF
SLABS = 32
CHUNK = 20
EPS = 1e-6
VMEM_BYTES = 24 * 2**20
F32 = jnp.float32
BF16 = jnp.bfloat16
NN = (((1,), (0,)), ((), ()))
NT = (((1,), (1,)), ((), ()))
TN = (((0,), (0,)), ((), ()))


def split(x):
    high = x.astype(BF16)
    low = (x - high.astype(F32)).astype(BF16)
    return high, low


def dot3(left, right, dims):
    def one(a, b):
        return lax.dot_general(a, b, dims, preferred_element_type=F32)

    return one(left[0], right[0]) + (one(left[0], right[1]) + one(left[1], right[0]))


def square3(parts):
    high, low = parts
    mixed = lax.dot_general(high, low, NN, preferred_element_type=F32)
    return lax.dot_general(high, high, NN, preferred_element_type=F32) + (mixed + jnp.transpose(mixed))


def call(kernel, name, out_shape, flops, **kwargs):
    return pl.pallas_call(
        kernel,
        out_shape=out_shape,
        compiler_params=pltpu.CompilerParams(vmem_limit_bytes=VMEM_BYTES),
        cost_estimate=pl.CostEstimate(flops=flops, bytes_accessed=2**22, transcendentals=0),
        name=name,
        **kwargs,
    )


VMEM = pl.BlockSpec(memory_space=pltpu.VMEM)
HBM = pl.BlockSpec(memory_space=pltpu.HBM)


def in_hbm(x):
    return pltpu.with_memory_space_constraint(x, pltpu.HBM)


def in_vmem(x):
    return pltpu.with_memory_space_constraint(x, pltpu.VMEM)


def row_tiles(ref, tile):
    return [pl.ds(start, tile) for start in range(0, ref.shape[0], tile)]


def outer3(e, o, dims):
    def one(a, b, dims):
        return lax.dot_general(a, b, dims, preferred_element_type=F32)

    mixed = one(e[0], e[1], NN) + one(o[0], o[1], dims)
    return (one(e[0], e[0], NN) + one(o[0], o[0], dims)) + (mixed + jnp.transpose(mixed))


def two_steps(e1, e2, o, eye):
    op, e1p, e2p = split(o), split(e1), split(e2)
    d1 = eye - outer3(e1p, op, NT)
    d2 = eye - outer3(e2p, op, TN)
    w1, w2 = weights(d1, d2, eye)
    w1, w2 = split(w1), split(w2)
    o = dot3(w1, op, NN)
    return dot3(w1, e1p, NN), dot3(w2, e2p, NN), o


def weights(d1, d2, eye):
    d1p, d2p = split(d1), split(d2)
    q1 = square3(d1p)
    q2 = square3(d2p)
    i1 = split(0.375 * eye + 0.3125 * d1 + 0.0625 * q1)
    i2 = split(0.375 * eye + 0.3125 * d2 + 0.0625 * q2)
    w1 = eye + 0.5 * d1 + dot3(split(q1), i1, NN)
    w2 = eye + 0.5 * d2 + dot3(split(q2), i2, NN)
    return w1, w2


def rotation_kernel(index, movers_ref, packed_ref, *outs):
    left = [packed_ref[CHUNK * k:CHUNK * k + 8, :] for k in range(SLABS)]
    right = [packed_ref[CHUNK * k + 8:CHUNK * k + 16, :] for k in range(SLABS)]
    cross = jnp.concatenate([jnp.concatenate(left, 0), jnp.concatenate(right, 0)], 1)
    norms = packed_ref[16:20, :]
    for k in range(1, SLABS):
        norms = norms + packed_ref[CHUNK * k + 16:CHUNK * k + 20, :]
    norm_a = jnp.concatenate([norms[0:1], norms[1:2]], 1)
    norm_m = jnp.concatenate([norms[2:3], norms[3:4]], 1)
    rows = lax.broadcasted_iota(jnp.int32, (HALF, HALF), 0)
    cols = lax.broadcasted_iota(jnp.int32, (HALF, HALF), 1)
    eye = (rows == cols).astype(F32)
    norm_a = jnp.transpose(jnp.broadcast_to(norm_a, (8, HALF)))[:, :1]
    diff = norm_a - norm_m
    total = norm_a + norm_m
    skew = -cross * diff / (diff * diff + 0.25 * total * total + EPS)
    scale = 1.0 / (4.0 * jnp.sqrt(PAIR + 2.0 * jnp.sum(skew * skew, keepdims=True)))
    start = scale * skew
    parts = split(start)
    own = (1.0 - scale * scale) * eye
    w1, w2 = weights(own - dot3(parts, parts, NT), own - dot3(parts, parts, TN), eye)
    e1, e2, o = scale * w1, scale * w2, dot3(split(w1), parts, NN)
    for _ in range(5):
        e1, e2, o = two_steps(e1, e2, o, eye)
    minus_ot = -jnp.transpose(o)

    firsts = movers_ref[index] == 1

    def put(move_a, move_m, stay_a, stay_m):
        if len(outs) == 2:
            for i, block in enumerate((move_a, move_m, stay_a, stay_m)):
                outs[0][HALF * i:HALF * i + HALF, :] = block
        else:
            outs[0][...], outs[1][...] = move_a, move_m
        outs[-1][:HALF, :] = stay_a
        outs[-1][HALF:, :] = stay_m

    @pl.when(firsts)
    def _():
        put(e1, minus_ot, o, e2)

    @pl.when(jnp.logical_not(firsts))
    def _():
        put(o, e2, e1, minus_ot)


def rotation(index, movers, packed, sizes):
    return call(
        lambda *refs: rotation_kernel(index, *refs),
        "rotation",
        [jax.ShapeDtypeStruct((n, HALF), F32) for n in sizes],
        10**10,
        in_specs=[pl.BlockSpec(memory_space=pltpu.SMEM), VMEM],
        out_specs=[VMEM] * len(sizes),
    )(movers, packed)


def pack(packed_ref, value):
    width = value.shape[1]
    per = 8 * width // 128
    for k in range(SLABS):
        for b in range(width // 128):
            packed_ref[per * k + 8 * b:per * k + 8 * b + 8, :] = value[8 * k:8 * k + 8, 128 * b:128 * b + 128]


def squares(x):
    return jnp.sum(x.reshape(-1, 8, x.shape[1]) ** 2, axis=0)


def first_kernel(x_ref, packed_ref, norm_ref):
    total, norm = 0.0, 0.0
    for rows in row_tiles(x_ref, 256):
        x = x_ref[rows, :]
        total += dot3(split(x[:, :HALF]), split(x[:, HALF:]), TN)
        norm += squares(x)
    pack(packed_ref, total)
    norm_ref[...] = jnp.concatenate([norm[:, :HALF], norm[:, HALF:]], 0)


def first_inner(x):
    return call(
        first_kernel,
        "first_inner",
        (jax.ShapeDtypeStruct((HALF * HALF // 128, 128), F32), jax.ShapeDtypeStruct((16, HALF), F32)),
        6 * x.shape[0] * HALF * HALF,
        in_specs=[VMEM],
        out_specs=[VMEM] * 2,
    )(in_vmem(x))


def meet_kernel(x_ref, q_ref, left_ref, a_ref, norm_ref, packed_ref):
    q = split(q_ref[...])
    norm, total = 0.0, 0.0
    for rows in row_tiles(x_ref, 512):
        a = dot3(split(x_ref[rows, :]), q, NN)
        a_ref[rows, :] = a
        norm += squares(a)
    norm_ref[...] = norm
    for rows in row_tiles(x_ref, 512):
        total += dot3(split(a_ref[rows, :]), split(left_ref[rows, :]), TN)
    pack(packed_ref, total)


def meet(x, q, left):
    rows = x.shape[0]
    return call(
        meet_kernel,
        "meet",
        (
            jax.ShapeDtypeStruct((rows, HALF), F32),
            jax.ShapeDtypeStruct((8, HALF), F32),
            jax.ShapeDtypeStruct((HALF * PAIR // 128, 128), F32),
        ),
        12 * rows * PAIR * HALF,
        in_specs=[VMEM] * 3,
        out_specs=[VMEM] * 3,
    )(in_vmem(x), q, in_vmem(left))


def fill(out_ref, cross, norm_a, norm_m):
    norm_a = jnp.sum(norm_a, axis=0, keepdims=True)
    norm_m = jnp.sum(norm_m, axis=0, keepdims=True)
    chunk = jnp.concatenate(
        [cross[:, :128], cross[:, 128:], norm_a[:, :128], norm_a[:, 128:], norm_m[:, :128], norm_m[:, 128:]], 0
    )
    for k in range(SLABS):
        out_ref[CHUNK * k:CHUNK * k + CHUNK, :] = chunk


def share_kernel(parts_ref, norm_ref, out_ref):
    total = parts_ref[0:16, :]
    for k in range(1, SLABS):
        total = total + parts_ref[16 * k:16 * k + 16, :]
    cross = jnp.concatenate([total[:8], total[8:]], 1)
    fill(out_ref, cross, norm_ref[:8, :], norm_ref[8:, :])


def project_kernel(parts_ref, high_ref, low_ref, norm_a_ref, norm_m_ref, out_ref):
    total = parts_ref[0:32, :]
    for k in range(1, SLABS):
        total = total + parts_ref[32 * k:32 * k + 32, :]
    wide = jnp.concatenate([total[8 * b:8 * b + 8] for b in range(4)], 1)
    wide = jnp.concatenate([wide, wide], 0)
    cross = dot3(split(wide), (high_ref[...], low_ref[...]), NN)[:8]
    fill(out_ref, cross, norm_a_ref[...], norm_m_ref[...])


def payload(kernel, *arrays):
    out = jax.ShapeDtypeStruct((SLABS * CHUNK, 128), F32)
    return call(kernel, "payload", out, 10**7, in_specs=[VMEM] * len(arrays), out_specs=VMEM)(*arrays)


def turn_kernel(
    x_ref, q_ref, out_ref, norm_ref, high_ref, low_ref, a_high_ref, a_low_ref, held_ref, turn_ref, part_ref, sems
):
    pltpu.sync_copy(q_ref, turn_ref)
    move, stay = split(turn_ref[:PAIR, :]), split(turn_ref[PAIR:, :])
    high_ref[...], low_ref[...] = move
    norm, outs = 0.0, []
    for i, rows in enumerate(row_tiles(x_ref, 512)):
        x = split(x_ref[rows, :])
        out = dot3(x, move, NN)
        held_ref[rows, :] = out
        norm += squares(out)
        part_ref[0, rows, :], part_ref[1, rows, :] = split(dot3(x, stay, NN))
        goes = ((held_ref, out_ref), (part_ref.at[0], a_high_ref), (part_ref.at[1], a_low_ref))
        for j, (here, there) in enumerate(goes):
            outs.append(pltpu.make_async_copy(here.at[rows], there.at[rows], sems.at[i, j]))
            outs[-1].start()
    norm_ref[...] = norm
    for copy in outs:
        copy.wait()


def turn(x, q):
    rows = x.shape[0]
    part = pltpu.HBM((rows, HALF), BF16)
    return call(
        turn_kernel,
        "turn",
        (
            pltpu.HBM((rows, HALF), F32),
            jax.ShapeDtypeStruct((8, HALF), F32),
            jax.ShapeDtypeStruct((PAIR, HALF), BF16),
            jax.ShapeDtypeStruct((PAIR, HALF), BF16),
            part,
            part,
        ),
        30 * 10**9,
        in_specs=[VMEM, HBM],
        out_specs=[HBM] + [VMEM] * 3 + [HBM] * 2,
        scratch_shapes=[
            pltpu.VMEM((rows, HALF), F32),
            pltpu.VMEM((2 * PAIR, HALF), F32),
            pltpu.VMEM((2, rows, HALF), BF16),
            pltpu.SemaphoreType.DMA((rows // 512, 3)),
        ],
    )(in_vmem(x), in_hbm(q))


def ready_kernel(m_ref, high_ref, low_ref):
    high_ref[...], low_ref[...] = split(m_ref[...])


def ready(m):
    out = jax.ShapeDtypeStruct(m.shape, BF16)
    return call(
        ready_kernel,
        "ready",
        (out, out),
        10**6,
        in_specs=[VMEM],
        out_specs=[VMEM] * 2,
    )(in_vmem(m))


def right_a_kernel(high_ref, low_ref, q_ref, out_ref):
    q = split(q_ref[...])
    for rows in row_tiles(high_ref, 512):
        out_ref[rows, :] = dot3((high_ref[rows, :], low_ref[rows, :]), q, NN)


def right_a(high, low, q):
    rows = high.shape[0]
    return call(
        right_a_kernel,
        "right_a",
        jax.ShapeDtypeStruct((rows, HALF), F32),
        6 * rows * HALF * HALF,
        in_specs=[VMEM] * 3,
        out_specs=VMEM,
    )(high, low, q)


def right_kernel(high_ref, low_ref, q_ref, part_ref, onto_ref, out_ref, held_ref, sems):
    q = split(q_ref[...])
    outs = []
    for i, rows in enumerate(row_tiles(high_ref, 512)):
        held_ref[rows, :] = part_ref[rows, :] + dot3((high_ref[rows, :], low_ref[rows, :]), q, NN)
        outs.append(pltpu.make_async_copy(held_ref.at[rows], out_ref.at[rows, pl.ds(HALF, HALF)], sems.at[i]))
        outs[-1].start()
    for copy in outs:
        copy.wait()


def right(high, low, q, part, onto):
    rows = high.shape[0]
    return call(
        right_kernel,
        "right",
        jax.ShapeDtypeStruct((rows, PAIR), F32),
        6 * rows * HALF * HALF,
        in_specs=[VMEM] * 4 + [HBM],
        out_specs=HBM,
        scratch_shapes=[pltpu.VMEM((rows, HALF), F32), pltpu.SemaphoreType.DMA((rows // 512,))],
        input_output_aliases={4: 0},
    )(high, low, q, part, onto)


def left_kernel(a_ref, m_ref, q_ref, out_ref, held_ref, sems):
    qa, qm = split(q_ref[:HALF, :]), split(q_ref[HALF:, :])
    outs = []
    for i, rows in enumerate(row_tiles(a_ref, 512)):
        held_ref[rows, :] = dot3(split(a_ref[rows, :]), qa, NN) + dot3(split(m_ref[rows, :]), qm, NN)
        outs.append(pltpu.make_async_copy(held_ref.at[rows], out_ref.at[rows, pl.ds(0, HALF)], sems.at[i]))
        outs[-1].start()
    for copy in outs:
        copy.wait()


def left(a, m, q):
    rows = a.shape[0]
    return call(
        left_kernel,
        "left",
        jax.ShapeDtypeStruct((rows, PAIR), F32),
        6 * rows * PAIR * HALF,
        in_specs=[VMEM] * 3,
        out_specs=HBM,
        scratch_shapes=[pltpu.VMEM((rows, HALF), F32), pltpu.SemaphoreType.DMA((rows // 512,))],
    )(a, in_vmem(m), q)


def passed_along(value):
    count = lax.axis_size("blk")
    return lax.ppermute(value, "blk", [(source, (source + 1) % count) for source in range(count)])


def exchanged(packed, shape):
    return lax.all_to_all(packed.reshape(SLABS, *shape), "slab", 0, 0).reshape(packed.shape)


def local(columns, movers):
    left_columns = passed_along(columns)

    cross, norms = first_inner(columns)
    movers, cross = lax.optimization_barrier((movers[:, 0], cross))
    parts = exchanged(cross, (16, 128))
    packed = exchanged(payload(share_kernel, parts, norms), (CHUNK // 2, 2, 128))
    both, stay = rotation(0, movers, packed, (2 * PAIR, PAIR))

    left_both = passed_along(both)
    a, norm_a, cross = meet(columns, stay, left_columns)
    parts = exchanged(cross, (32, 128))
    m, norm_m, high, low, *left_a = turn(left_columns, left_both)
    left_m = passed_along(m)
    packed = exchanged(payload(project_kernel, parts, high, low, norm_a, norm_m), (CHUNK // 2, 2, 128))
    move_a, move_m, stay = rotation(1, movers, packed, (HALF, HALF, PAIR))

    left_move_a = passed_along(move_a)
    left_move_m = passed_along(move_m)
    left_m = ready(left_m)
    out = left(a, m, stay)
    left_a, left_m, out = lax.optimization_barrier((left_a, left_m, out))
    part = right_a(*left_a, left_move_a)
    return right(*left_m, left_move_m, part, out)


def solution(mesh):
    placed = (P("slab", "blk"), P(None, "blk"))
    return jax.shard_map(
        local, mesh=mesh, in_specs=placed, out_specs=P("slab", "blk"), check_vma=False
    )
```

```python
import jax
import jax.numpy as jnp
from jax import lax
from jax.experimental import pallas as pl
from jax.experimental.pallas import tpu as pltpu
from jax.sharding import PartitionSpec as P

HALF = 256
PAIR = 2 * HALF
SLABS = 32
CHUNK = 20
FIRST = 17
EPS = 1e-6
VMEM_BYTES = 24 * 2**20
F32 = jnp.float32
BF16 = jnp.bfloat16
NN = (((1,), (0,)), ((), ()))
NT = (((1,), (1,)), ((), ()))
TN = (((0,), (0,)), ((), ()))


def split(x):
    high = x.astype(BF16)
    low = (x - high.astype(F32)).astype(BF16)
    return high, low


def dot3(left, right, dims):
    def one(a, b):
        return lax.dot_general(a, b, dims, preferred_element_type=F32)

    return one(left[0], right[0]) + (one(left[0], right[1]) + one(left[1], right[0]))


def square3(parts):
    high, low = parts
    mixed = lax.dot_general(high, low, NN, preferred_element_type=F32)
    return lax.dot_general(high, high, NN, preferred_element_type=F32) + (mixed + jnp.transpose(mixed))


def call(kernel, name, out_shape, flops, **kwargs):
    return pl.pallas_call(
        kernel,
        out_shape=out_shape,
        compiler_params=pltpu.CompilerParams(vmem_limit_bytes=VMEM_BYTES),
        cost_estimate=pl.CostEstimate(flops=flops, bytes_accessed=2**22, transcendentals=0),
        name=name,
        **kwargs,
    )


VMEM = pl.BlockSpec(memory_space=pltpu.VMEM)
HBM = pl.BlockSpec(memory_space=pltpu.HBM)


def in_hbm(x):
    return pltpu.with_memory_space_constraint(x, pltpu.HBM)


def in_vmem(x):
    return pltpu.with_memory_space_constraint(x, pltpu.VMEM)


def row_tiles(ref, tile):
    return [pl.ds(start, tile) for start in range(0, ref.shape[0], tile)]


def outer3(e, o, dims):
    def one(a, b, dims):
        return lax.dot_general(a, b, dims, preferred_element_type=F32)

    mixed = one(e[0], e[1], NN) + one(o[0], o[1], dims)
    return (one(e[0], e[0], NN) + one(o[0], o[0], dims)) + (mixed + jnp.transpose(mixed))


def two_steps(e1, e2, o, eye):
    op, e1p, e2p = split(o), split(e1), split(e2)
    d1 = eye - outer3(e1p, op, NT)
    d2 = eye - outer3(e2p, op, TN)
    w1, w2 = weights(d1, d2, eye)
    w1, w2 = split(w1), split(w2)
    o = dot3(w1, op, NN)
    return dot3(w1, e1p, NN), dot3(w2, e2p, NN), o


def weights(d1, d2, eye):
    d1p, d2p = split(d1), split(d2)
    q1 = square3(d1p)
    q2 = square3(d2p)
    i1 = split(0.375 * eye + 0.3125 * d1 + 0.0625 * q1)
    i2 = split(0.375 * eye + 0.3125 * d2 + 0.0625 * q2)
    w1 = eye + 0.5 * d1 + dot3(split(q1), i1, NN)
    w2 = eye + 0.5 * d2 + dot3(split(q2), i2, NN)
    return w1, w2


def rotation_kernel(index, movers_ref, packed_ref, *outs):
    chunk = packed_ref.shape[0] // SLABS
    left = [packed_ref[chunk * k:chunk * k + 8, :] for k in range(SLABS)]
    right = [packed_ref[chunk * k + 8:chunk * k + 16, :] for k in range(SLABS)]
    cross = jnp.concatenate([jnp.concatenate(left, 0), jnp.concatenate(right, 0)], 1)
    if chunk == FIRST:
        norms = jnp.concatenate([packed_ref[FIRST * k + 16:FIRST * k + 17, :] for k in range(4)], 0)
    else:
        norms = packed_ref[16:20, :]
        for k in range(1, SLABS):
            norms = norms + packed_ref[CHUNK * k + 16:CHUNK * k + 20, :]
    norm_a = jnp.concatenate([norms[0:1], norms[1:2]], 1)
    norm_m = jnp.concatenate([norms[2:3], norms[3:4]], 1)
    rows = lax.broadcasted_iota(jnp.int32, (HALF, HALF), 0)
    cols = lax.broadcasted_iota(jnp.int32, (HALF, HALF), 1)
    eye = (rows == cols).astype(F32)
    norm_a = jnp.transpose(jnp.broadcast_to(norm_a, (8, HALF)))[:, :1]
    diff = norm_a - norm_m
    total = norm_a + norm_m
    skew = -cross * diff / (diff * diff + 0.25 * total * total + EPS)
    scale = 1.0 / (4.0 * jnp.sqrt(PAIR + 2.0 * jnp.sum(skew * skew, keepdims=True)))
    start = scale * skew
    parts = split(start)
    own = (1.0 - scale * scale) * eye
    w1, w2 = weights(own - dot3(parts, parts, NT), own - dot3(parts, parts, TN), eye)
    e1, e2, o = scale * w1, scale * w2, dot3(split(w1), parts, NN)
    for _ in range(5):
        e1, e2, o = two_steps(e1, e2, o, eye)
    minus_ot = -jnp.transpose(o)

    firsts = movers_ref[index] == 1

    def put(move_a, move_m, stay_a, stay_m):
        if len(outs) == 2:
            for i, block in enumerate((move_a, move_m, stay_a, stay_m)):
                outs[0][HALF * i:HALF * i + HALF, :] = block
        else:
            outs[0][...], outs[1][...] = move_a, move_m
        outs[-1][:HALF, :] = stay_a
        outs[-1][HALF:, :] = stay_m

    @pl.when(firsts)
    def _():
        put(e1, minus_ot, o, e2)

    @pl.when(jnp.logical_not(firsts))
    def _():
        put(o, e2, e1, minus_ot)


def rotation(index, movers, packed, sizes):
    return call(
        lambda *refs: rotation_kernel(index, *refs),
        "rotation",
        [jax.ShapeDtypeStruct((n, HALF), F32) for n in sizes],
        10**10,
        in_specs=[pl.BlockSpec(memory_space=pltpu.SMEM), VMEM],
        out_specs=[VMEM] * len(sizes),
    )(movers, packed)


def pack(packed_ref, value):
    width = value.shape[1]
    per = 8 * width // 128
    for k in range(SLABS):
        for b in range(width // 128):
            packed_ref[per * k + 8 * b:per * k + 8 * b + 8, :] = value[8 * k:8 * k + 8, 128 * b:128 * b + 128]


def squares(x):
    return jnp.sum(x.reshape(-1, 8, x.shape[1]) ** 2, axis=0)


def first_kernel(x_ref, packed_ref):
    total, norm = 0.0, 0.0
    for rows in row_tiles(x_ref, 256):
        x = x_ref[rows, :]
        total += dot3(split(x[:, :HALF]), split(x[:, HALF:]), TN)
        norm += squares(x)
    norm = jnp.sum(norm, axis=0, keepdims=True)
    for k in range(SLABS):
        packed_ref[FIRST * k:FIRST * k + 8, :] = total[8 * k:8 * k + 8, :128]
        packed_ref[FIRST * k + 8:FIRST * k + 16, :] = total[8 * k:8 * k + 8, 128:]
        packed_ref[FIRST * k + 16:FIRST * k + 17, :] = norm[:, 128 * (k % 4):128 * (k % 4) + 128]


def first_inner(x):
    return call(
        first_kernel,
        "first_inner",
        jax.ShapeDtypeStruct((SLABS * FIRST, 128), F32),
        6 * x.shape[0] * HALF * HALF,
        in_specs=[VMEM],
        out_specs=VMEM,
    )(in_vmem(x))


def meet_kernel(x_ref, q_ref, left_ref, a_ref, norm_ref, packed_ref):
    q = split(q_ref[...])
    norm, total = 0.0, 0.0
    for rows in row_tiles(x_ref, 512):
        a = dot3(split(x_ref[rows, :]), q, NN)
        a_ref[rows, :] = a
        norm += squares(a)
    norm_ref[...] = norm
    for rows in row_tiles(x_ref, 512):
        total += dot3(split(a_ref[rows, :]), split(left_ref[rows, :]), TN)
    pack(packed_ref, total)


def meet(x, q, left):
    rows = x.shape[0]
    return call(
        meet_kernel,
        "meet",
        (
            jax.ShapeDtypeStruct((rows, HALF), F32),
            jax.ShapeDtypeStruct((8, HALF), F32),
            jax.ShapeDtypeStruct((HALF * PAIR // 128, 128), F32),
        ),
        12 * rows * PAIR * HALF,
        in_specs=[VMEM] * 3,
        out_specs=[VMEM] * 3,
    )(in_vmem(x), q, in_vmem(left))


def fill(out_ref, cross, norm_a, norm_m):
    norm_a = jnp.sum(norm_a, axis=0, keepdims=True)
    norm_m = jnp.sum(norm_m, axis=0, keepdims=True)
    chunk = jnp.concatenate(
        [cross[:, :128], cross[:, 128:], norm_a[:, :128], norm_a[:, 128:], norm_m[:, :128], norm_m[:, 128:]], 0
    )
    for k in range(SLABS):
        out_ref[CHUNK * k:CHUNK * k + CHUNK, :] = chunk


def share_kernel(parts_ref, out_ref):
    total = parts_ref[:FIRST, :]
    for k in range(1, SLABS):
        total = total + parts_ref[FIRST * k:FIRST * k + FIRST, :]
    for k in range(SLABS):
        out_ref[FIRST * k:FIRST * k + FIRST, :] = total


def project_kernel(parts_ref, high_ref, low_ref, norm_a_ref, norm_m_ref, out_ref):
    total = parts_ref[0:32, :]
    for k in range(1, SLABS):
        total = total + parts_ref[32 * k:32 * k + 32, :]
    wide = jnp.concatenate([total[8 * b:8 * b + 8] for b in range(4)], 1)
    wide = jnp.concatenate([wide, wide], 0)
    cross = dot3(split(wide), (high_ref[...], low_ref[...]), NN)[:8]
    fill(out_ref, cross, norm_a_ref[...], norm_m_ref[...])


def payload(kernel, chunk, *arrays):
    out = jax.ShapeDtypeStruct((SLABS * chunk, 128), F32)
    return call(kernel, "payload", out, 10**7, in_specs=[VMEM] * len(arrays), out_specs=VMEM)(*arrays)


def turn_kernel(
    x_ref, q_ref, out_ref, norm_ref, high_ref, low_ref, a_high_ref, a_low_ref, held_ref, turn_ref, part_ref, sems
):
    pltpu.sync_copy(q_ref, turn_ref)
    move, stay = split(turn_ref[:PAIR, :]), split(turn_ref[PAIR:, :])
    high_ref[...], low_ref[...] = move
    norm, outs = 0.0, []
    for i, rows in enumerate(row_tiles(x_ref, 512)):
        x = split(x_ref[rows, :])
        out = dot3(x, move, NN)
        held_ref[rows, :] = out
        norm += squares(out)
        part_ref[0, rows, :], part_ref[1, rows, :] = split(dot3(x, stay, NN))
        goes = ((held_ref, out_ref), (part_ref.at[0], a_high_ref), (part_ref.at[1], a_low_ref))
        for j, (here, there) in enumerate(goes):
            outs.append(pltpu.make_async_copy(here.at[rows], there.at[rows], sems.at[i, j]))
            outs[-1].start()
    norm_ref[...] = norm
    for copy in outs:
        copy.wait()


def turn(x, q):
    rows = x.shape[0]
    part = pltpu.HBM((rows, HALF), BF16)
    return call(
        turn_kernel,
        "turn",
        (
            pltpu.HBM((rows, HALF), F32),
            jax.ShapeDtypeStruct((8, HALF), F32),
            jax.ShapeDtypeStruct((PAIR, HALF), BF16),
            jax.ShapeDtypeStruct((PAIR, HALF), BF16),
            part,
            part,
        ),
        30 * 10**9,
        in_specs=[VMEM, HBM],
        out_specs=[HBM] + [VMEM] * 3 + [HBM] * 2,
        scratch_shapes=[
            pltpu.VMEM((rows, HALF), F32),
            pltpu.VMEM((2 * PAIR, HALF), F32),
            pltpu.VMEM((2, rows, HALF), BF16),
            pltpu.SemaphoreType.DMA((rows // 512, 3)),
        ],
    )(in_vmem(x), in_hbm(q))


def ready_kernel(m_ref, high_ref, low_ref):
    high_ref[...], low_ref[...] = split(m_ref[...])


def ready(m):
    out = jax.ShapeDtypeStruct(m.shape, BF16)
    return call(
        ready_kernel,
        "ready",
        (out, out),
        10**6,
        in_specs=[VMEM],
        out_specs=[VMEM] * 2,
    )(in_vmem(m))


def right_a_kernel(high_ref, low_ref, q_ref, out_ref):
    q = split(q_ref[...])
    for rows in row_tiles(high_ref, 512):
        out_ref[rows, :] = dot3((high_ref[rows, :], low_ref[rows, :]), q, NN)


def right_a(high, low, q):
    rows = high.shape[0]
    return call(
        right_a_kernel,
        "right_a",
        jax.ShapeDtypeStruct((rows, HALF), F32),
        6 * rows * HALF * HALF,
        in_specs=[VMEM] * 3,
        out_specs=VMEM,
    )(high, low, q)


def right_kernel(high_ref, low_ref, q_ref, part_ref, onto_ref, out_ref, held_ref, sems):
    q = split(q_ref[...])
    outs = []
    for i, rows in enumerate(row_tiles(high_ref, 512)):
        held_ref[rows, :] = part_ref[rows, :] + dot3((high_ref[rows, :], low_ref[rows, :]), q, NN)
        outs.append(pltpu.make_async_copy(held_ref.at[rows], out_ref.at[rows, pl.ds(HALF, HALF)], sems.at[i]))
        outs[-1].start()
    for copy in outs:
        copy.wait()


def right(high, low, q, part, onto):
    rows = high.shape[0]
    return call(
        right_kernel,
        "right",
        jax.ShapeDtypeStruct((rows, PAIR), F32),
        6 * rows * HALF * HALF,
        in_specs=[VMEM] * 4 + [HBM],
        out_specs=HBM,
        scratch_shapes=[pltpu.VMEM((rows, HALF), F32), pltpu.SemaphoreType.DMA((rows // 512,))],
        input_output_aliases={4: 0},
    )(high, low, q, part, onto)


def left_kernel(a_ref, m_ref, q_ref, out_ref, held_ref, sems):
    qa, qm = split(q_ref[:HALF, :]), split(q_ref[HALF:, :])
    outs = []
    for i, rows in enumerate(row_tiles(a_ref, 512)):
        held_ref[rows, :] = dot3(split(a_ref[rows, :]), qa, NN) + dot3(split(m_ref[rows, :]), qm, NN)
        outs.append(pltpu.make_async_copy(held_ref.at[rows], out_ref.at[rows, pl.ds(0, HALF)], sems.at[i]))
        outs[-1].start()
    for copy in outs:
        copy.wait()


def left(a, m, q):
    rows = a.shape[0]
    return call(
        left_kernel,
        "left",
        jax.ShapeDtypeStruct((rows, PAIR), F32),
        6 * rows * PAIR * HALF,
        in_specs=[VMEM] * 3,
        out_specs=HBM,
        scratch_shapes=[pltpu.VMEM((rows, HALF), F32), pltpu.SemaphoreType.DMA((rows // 512,))],
    )(a, in_vmem(m), q)


def passed_along(value):
    count = lax.axis_size("blk")
    return lax.ppermute(value, "blk", [(source, (source + 1) % count) for source in range(count)])


def exchanged(packed, shape):
    return lax.all_to_all(packed.reshape(SLABS, *shape), "slab", 0, 0).reshape(packed.shape)


def local(columns, movers):
    left_columns = passed_along(columns)

    cross = first_inner(columns)
    movers, cross = lax.optimization_barrier((movers[:, 0], cross))
    parts = exchanged(cross, (FIRST, 1, 128))
    packed = exchanged(payload(share_kernel, FIRST, parts), (FIRST, 1, 128))
    both, stay = rotation(0, movers, packed, (2 * PAIR, PAIR))

    left_both = passed_along(both)
    a, norm_a, cross = meet(columns, stay, left_columns)
    parts = exchanged(cross, (32, 128))
    m, norm_m, high, low, *left_a = turn(left_columns, left_both)
    left_m = passed_along(m)
    packed = exchanged(payload(project_kernel, CHUNK, parts, high, low, norm_a, norm_m), (CHUNK // 2, 2, 128))
    move_a, move_m, stay = rotation(1, movers, packed, (HALF, HALF, PAIR))

    left_move_a = passed_along(move_a)
    left_move_m = passed_along(move_m)
    left_m = ready(left_m)
    out = left(a, m, stay)
    left_a, left_m, out = lax.optimization_barrier((left_a, left_m, out))
    part = right_a(*left_a, left_move_a)
    return right(*left_m, left_move_m, part, out)


def solution(mesh):
    placed = (P("slab", "blk"), P(None, "blk"))
    return jax.shard_map(
        local, mesh=mesh, in_specs=placed, out_specs=P("slab", "blk"), check_vma=False
    )
```

```python
import jax
import jax.numpy as jnp
from jax import lax
from jax.experimental import pallas as pl
from jax.experimental.pallas import tpu as pltpu
from jax.sharding import PartitionSpec as P

HALF = 256
PAIR = 2 * HALF
SLABS = 32
CHUNK = 20
EPS = 1e-6
VMEM_BYTES = 24 * 2**20
F32 = jnp.float32
BF16 = jnp.bfloat16
NN = (((1,), (0,)), ((), ()))
NT = (((1,), (1,)), ((), ()))
TN = (((0,), (0,)), ((), ()))


def split(x):
    high = x.astype(BF16)
    low = (x - high.astype(F32)).astype(BF16)
    return high, low


def dot3(left, right, dims):
    def one(a, b):
        return lax.dot_general(a, b, dims, preferred_element_type=F32)

    return one(left[0], right[0]) + (one(left[0], right[1]) + one(left[1], right[0]))


def square3(parts):
    high, low = parts
    mixed = lax.dot_general(high, low, NN, preferred_element_type=F32)
    return lax.dot_general(high, high, NN, preferred_element_type=F32) + (mixed + jnp.transpose(mixed))


def call(kernel, name, out_shape, flops, **kwargs):
    return pl.pallas_call(
        kernel,
        out_shape=out_shape,
        compiler_params=pltpu.CompilerParams(vmem_limit_bytes=VMEM_BYTES),
        cost_estimate=pl.CostEstimate(flops=flops, bytes_accessed=2**22, transcendentals=0),
        name=name,
        **kwargs,
    )


VMEM = pl.BlockSpec(memory_space=pltpu.VMEM)
HBM = pl.BlockSpec(memory_space=pltpu.HBM)


def in_hbm(x):
    return pltpu.with_memory_space_constraint(x, pltpu.HBM)


def in_vmem(x):
    return pltpu.with_memory_space_constraint(x, pltpu.VMEM)


def row_tiles(ref, tile):
    return [pl.ds(start, tile) for start in range(0, ref.shape[0], tile)]


def outer3(e, o, dims):
    def one(a, b, dims):
        return lax.dot_general(a, b, dims, preferred_element_type=F32)

    mixed = one(e[0], e[1], NN) + one(o[0], o[1], dims)
    return (one(e[0], e[0], NN) + one(o[0], o[0], dims)) + (mixed + jnp.transpose(mixed))


def two_steps(e1, e2, o, eye):
    op, e1p, e2p = split(o), split(e1), split(e2)
    d1 = eye - outer3(e1p, op, NT)
    d2 = eye - outer3(e2p, op, TN)
    w1, w2 = weights(d1, d2, eye)
    w1, w2 = split(w1), split(w2)
    o = dot3(w1, op, NN)
    return dot3(w1, e1p, NN), dot3(w2, e2p, NN), o


def weights(d1, d2, eye):
    d1p, d2p = split(d1), split(d2)
    q1 = square3(d1p)
    q2 = square3(d2p)
    i1 = split(0.375 * eye + 0.3125 * d1 + 0.0625 * q1)
    i2 = split(0.375 * eye + 0.3125 * d2 + 0.0625 * q2)
    w1 = eye + 0.5 * d1 + dot3(split(q1), i1, NN)
    w2 = eye + 0.5 * d2 + dot3(split(q2), i2, NN)
    return w1, w2


def rotation_kernel(index, movers_ref, packed_ref, *outs):
    left = [packed_ref[CHUNK * k:CHUNK * k + 8, :] for k in range(SLABS)]
    right = [packed_ref[CHUNK * k + 8:CHUNK * k + 16, :] for k in range(SLABS)]
    cross = jnp.concatenate([jnp.concatenate(left, 0), jnp.concatenate(right, 0)], 1)
    norms = packed_ref[16:20, :]
    for k in range(1, SLABS):
        norms = norms + packed_ref[CHUNK * k + 16:CHUNK * k + 20, :]
    norm_a = jnp.concatenate([norms[0:1], norms[1:2]], 1)
    norm_m = jnp.concatenate([norms[2:3], norms[3:4]], 1)
    rows = lax.broadcasted_iota(jnp.int32, (HALF, HALF), 0)
    cols = lax.broadcasted_iota(jnp.int32, (HALF, HALF), 1)
    eye = (rows == cols).astype(F32)
    norm_a = jnp.transpose(jnp.broadcast_to(norm_a, (8, HALF)))[:, :1]
    diff = norm_a - norm_m
    total = norm_a + norm_m
    skew = -cross * diff / (diff * diff + 0.25 * total * total + EPS)
    scale = 1.0 / (4.0 * jnp.sqrt(PAIR + 2.0 * jnp.sum(skew * skew, keepdims=True)))
    start = scale * skew
    parts = split(start)
    own = (1.0 - scale * scale) * eye
    w1, w2 = weights(own - dot3(parts, parts, NT), own - dot3(parts, parts, TN), eye)
    e1, e2, o = scale * w1, scale * w2, dot3(split(w1), parts, NN)
    for _ in range(5):
        e1, e2, o = two_steps(e1, e2, o, eye)
    minus_ot = -jnp.transpose(o)

    firsts = movers_ref[index] == 1

    def put(move_a, move_m, stay_a, stay_m):
        if len(outs) == 2:
            outs[0][:HALF, :] = move_a
            outs[0][HALF:, :] = move_m
        else:
            outs[0][...], outs[1][...] = move_a, move_m
        outs[-1][:HALF, :] = stay_a
        outs[-1][HALF:, :] = stay_m

    @pl.when(firsts)
    def _():
        put(e1, minus_ot, o, e2)

    @pl.when(jnp.logical_not(firsts))
    def _():
        put(o, e2, e1, minus_ot)


def rotation(index, movers, packed, sizes):
    return call(
        lambda *refs: rotation_kernel(index, *refs),
        "rotation",
        [jax.ShapeDtypeStruct((n, HALF), F32) for n in sizes],
        10**10,
        in_specs=[pl.BlockSpec(memory_space=pltpu.SMEM), VMEM],
        out_specs=[VMEM] * len(sizes),
    )(movers, packed)


def pack(packed_ref, value):
    width = value.shape[1]
    per = 8 * width // 128
    for k in range(SLABS):
        for b in range(width // 128):
            packed_ref[per * k + 8 * b:per * k + 8 * b + 8, :] = value[8 * k:8 * k + 8, 128 * b:128 * b + 128]


def squares(x):
    return jnp.sum(x.reshape(-1, 8, x.shape[1]) ** 2, axis=0)


def first_kernel(x_ref, packed_ref, norm_ref):
    total, norm = 0.0, 0.0
    for rows in row_tiles(x_ref, 256):
        x = x_ref[rows, :]
        total += dot3(split(x[:, :HALF]), split(x[:, HALF:]), TN)
        norm += squares(x)
    pack(packed_ref, total)
    norm_ref[...] = jnp.concatenate([norm[:, :HALF], norm[:, HALF:]], 0)


def first_inner(x):
    return call(
        first_kernel,
        "first_inner",
        (jax.ShapeDtypeStruct((HALF * HALF // 128, 128), F32), jax.ShapeDtypeStruct((16, HALF), F32)),
        6 * x.shape[0] * HALF * HALF,
        in_specs=[VMEM],
        out_specs=[VMEM] * 2,
    )(in_vmem(x))


def meet_kernel(x_ref, q_ref, left_ref, a_ref, norm_ref, packed_ref, held_ref, sems):
    q = split(q_ref[...])
    norm, total, outs = 0.0, 0.0, []
    for i, rows in enumerate(row_tiles(x_ref, 512)):
        a = dot3(split(x_ref[rows, :]), q, NN)
        held_ref[rows, :] = a
        norm += squares(a)
        outs.append(pltpu.make_async_copy(held_ref.at[rows], a_ref.at[rows], sems.at[i]))
        outs[-1].start()
    norm_ref[...] = norm
    for rows in row_tiles(x_ref, 512):
        total += dot3(split(held_ref[rows, :]), split(left_ref[rows, :]), TN)
    pack(packed_ref, total)
    for copy in outs:
        copy.wait()


def meet(x, q, left):
    rows = x.shape[0]
    return call(
        meet_kernel,
        "meet",
        (
            pltpu.HBM((rows, HALF), F32),
            jax.ShapeDtypeStruct((8, HALF), F32),
            jax.ShapeDtypeStruct((HALF * PAIR // 128, 128), F32),
        ),
        12 * rows * PAIR * HALF,
        in_specs=[VMEM] * 3,
        out_specs=[HBM, VMEM, VMEM],
        scratch_shapes=[pltpu.VMEM((rows, HALF), F32), pltpu.SemaphoreType.DMA((rows // 512,))],
    )(in_vmem(x), q, in_vmem(left))


def fill(out_ref, cross, norm_a, norm_m):
    norm_a = jnp.sum(norm_a, axis=0, keepdims=True)
    norm_m = jnp.sum(norm_m, axis=0, keepdims=True)
    chunk = jnp.concatenate(
        [cross[:, :128], cross[:, 128:], norm_a[:, :128], norm_a[:, 128:], norm_m[:, :128], norm_m[:, 128:]], 0
    )
    for k in range(SLABS):
        out_ref[CHUNK * k:CHUNK * k + CHUNK, :] = chunk


def share_kernel(parts_ref, norm_ref, out_ref):
    total = parts_ref[0:16, :]
    for k in range(1, SLABS):
        total = total + parts_ref[16 * k:16 * k + 16, :]
    cross = jnp.concatenate([total[:8], total[8:]], 1)
    fill(out_ref, cross, norm_ref[:8, :], norm_ref[8:, :])


def project_kernel(parts_ref, move_ref, norm_a_ref, norm_m_ref, out_ref, held_ref, sem):
    copy = pltpu.make_async_copy(move_ref, held_ref, sem)
    copy.start()
    total = parts_ref[0:32, :]
    for k in range(1, SLABS):
        total = total + parts_ref[32 * k:32 * k + 32, :]
    wide = jnp.concatenate([total[8 * b:8 * b + 8] for b in range(4)], 1)
    wide = jnp.concatenate([wide, wide], 0)
    copy.wait()
    cross = dot3(split(wide), split(held_ref[...]), NN)[:8]
    fill(out_ref, cross, norm_a_ref[...], norm_m_ref[...])


def share(parts, norms):
    out = jax.ShapeDtypeStruct((SLABS * CHUNK, 128), F32)
    return call(share_kernel, "share", out, 10**7, in_specs=[VMEM] * 2, out_specs=VMEM)(parts, norms)


def project(parts, move, norm_a, norm_m):
    return call(
        project_kernel,
        "project",
        jax.ShapeDtypeStruct((SLABS * CHUNK, 128), F32),
        10**7,
        in_specs=[VMEM, HBM, VMEM, VMEM],
        out_specs=VMEM,
        scratch_shapes=[pltpu.VMEM((PAIR, HALF), F32), pltpu.SemaphoreType.DMA],
    )(parts, in_hbm(move), norm_a, norm_m)


def turn_kernel(x_ref, q_ref, stay_ref, out_ref, norm_ref, held_ref, sems):
    rows = x_ref.shape[0]
    outs = [pltpu.make_async_copy(stay_ref, out_ref.at[pl.ds(rows, PAIR)], sems.at[rows // 512])]
    outs[0].start()
    q = split(q_ref[...])
    norm = 0.0
    for i, part in enumerate(row_tiles(x_ref, 512)):
        out = dot3(split(x_ref[part, :]), q, NN)
        held_ref[part, :] = out
        norm += squares(out)
        outs.append(pltpu.make_async_copy(held_ref.at[part], out_ref.at[part], sems.at[i]))
        outs[-1].start()
    norm_ref[...] = norm
    for copy in outs:
        copy.wait()


def turn(x, q, stay):
    rows = x.shape[0]
    return call(
        turn_kernel,
        "turn",
        (
            pltpu.HBM((rows + PAIR, HALF), F32),
            jax.ShapeDtypeStruct((8, HALF), F32),
        ),
        6 * rows * PAIR * HALF,
        in_specs=[VMEM] * 3,
        out_specs=[HBM, VMEM],
        scratch_shapes=[pltpu.VMEM((rows, HALF), F32), pltpu.SemaphoreType.DMA((rows // 512 + 1,))],
    )(in_vmem(x), q, in_vmem(stay))


def ready_kernel(x_ref, m_ref, a_high_ref, a_low_ref, m_high_ref, m_low_ref):
    q = split(m_ref[x_ref.shape[0]:, :])
    for rows in row_tiles(x_ref, 512):
        m_high_ref[rows, :], m_low_ref[rows, :] = split(m_ref[rows, :])
        out = dot3(split(x_ref[rows, :]), q, NN)
        a_high_ref[rows, :], a_low_ref[rows, :] = split(out)


def ready(x, m):
    rows = x.shape[0]
    out = jax.ShapeDtypeStruct((rows, HALF), BF16)
    parts = call(
        ready_kernel,
        "ready",
        (out,) * 4,
        10**6,
        in_specs=[VMEM] * 2,
        out_specs=[VMEM] * 4,
    )(in_vmem(x), in_vmem(m))
    return parts[:2], parts[2:]


def right_a_kernel(high_ref, low_ref, q_ref, out_ref):
    q = split(q_ref[...])
    for rows in row_tiles(high_ref, 512):
        out_ref[rows, :] = dot3((high_ref[rows, :], low_ref[rows, :]), q, NN)


def right_a(high, low, q):
    rows = high.shape[0]
    return call(
        right_a_kernel,
        "right_a",
        jax.ShapeDtypeStruct((rows, HALF), F32),
        6 * rows * HALF * HALF,
        in_specs=[VMEM] * 3,
        out_specs=VMEM,
    )(high, low, q)


def right_kernel(high_ref, low_ref, q_ref, part_ref, onto_ref, out_ref, held_ref, sems):
    q = split(q_ref[...])
    outs = []
    for i, rows in enumerate(row_tiles(high_ref, 512)):
        held_ref[rows, :] = part_ref[rows, :] + dot3((high_ref[rows, :], low_ref[rows, :]), q, NN)
        outs.append(pltpu.make_async_copy(held_ref.at[rows], out_ref.at[rows, pl.ds(HALF, HALF)], sems.at[i]))
        outs[-1].start()
    for copy in outs:
        copy.wait()


def right(high, low, q, part, onto):
    rows = high.shape[0]
    return call(
        right_kernel,
        "right",
        jax.ShapeDtypeStruct((rows, PAIR), F32),
        6 * rows * HALF * HALF,
        in_specs=[VMEM] * 4 + [HBM],
        out_specs=HBM,
        scratch_shapes=[pltpu.VMEM((rows, HALF), F32), pltpu.SemaphoreType.DMA((rows // 512,))],
        input_output_aliases={4: 0},
    )(high, low, q, part, onto)


def left_kernel(a_ref, m_ref, q_ref, out_ref, held_ref, sems):
    qa, qm = split(q_ref[:HALF, :]), split(q_ref[HALF:, :])
    outs = []
    for i, rows in enumerate(row_tiles(a_ref, 512)):
        held_ref[rows, :] = dot3(split(a_ref[rows, :]), qa, NN) + dot3(split(m_ref[rows, :]), qm, NN)
        outs.append(pltpu.make_async_copy(held_ref.at[rows], out_ref.at[rows, pl.ds(0, HALF)], sems.at[i]))
        outs[-1].start()
    for copy in outs:
        copy.wait()


def left(a, m, q):
    rows = a.shape[0]
    return call(
        left_kernel,
        "left",
        jax.ShapeDtypeStruct((rows, PAIR), F32),
        6 * rows * PAIR * HALF,
        in_specs=[VMEM] * 3,
        out_specs=HBM,
        scratch_shapes=[pltpu.VMEM((rows, HALF), F32), pltpu.SemaphoreType.DMA((rows // 512,))],
    )(in_vmem(a), in_vmem(m), q)


def passed_along(value):
    count = lax.axis_size("blk")
    return lax.ppermute(value, "blk", [(source, (source + 1) % count) for source in range(count)])


def exchanged(packed, shape):
    return lax.all_to_all(packed.reshape(SLABS, *shape), "slab", 0, 0).reshape(packed.shape)


def local(columns, movers):
    left_columns = passed_along(columns)

    cross, norms = first_inner(columns)
    movers, cross = lax.optimization_barrier((movers[:, 0], cross))
    parts = exchanged(cross, (16, 128))
    packed = exchanged(share(parts, norms), (CHUNK // 2, 2, 128))
    move, stay = rotation(0, movers, packed, (PAIR, PAIR))

    left_move = passed_along(move)
    a, norm_a, cross = meet(columns, stay, left_columns)
    parts = exchanged(cross, (16, 2, 128))
    m, norm_m = turn(left_columns, left_move, stay)
    left_m = passed_along(m)
    packed = exchanged(project(parts, left_move, norm_a, norm_m), (CHUNK // 2, 2, 128))
    move_a, move_m, stay = rotation(1, movers, packed, (HALF, HALF, PAIR))

    left_move_m = passed_along(move_m)
    left_move_a = passed_along(move_a)
    left_a, left_m = ready(left_columns, left_m)
    out = left(a, m, stay)
    left_a, left_m, out = lax.optimization_barrier((left_a, left_m, out))
    part = right_a(*left_a, left_move_a)
    return right(*left_m, left_move_m, part, out)


def solution(mesh):
    placed = (P("slab", "blk"), P(None, "blk"))
    return jax.shard_map(
        local, mesh=mesh, in_specs=placed, out_specs=P("slab", "blk"), check_vma=False
    )
```

```python
import jax
import jax.numpy as jnp
from jax import lax
from jax.experimental import pallas as pl
from jax.experimental.pallas import tpu as pltpu
from jax.sharding import PartitionSpec as P

HALF = 256
PAIR = 2 * HALF
SLABS = 32
CHUNK = 20
EPS = 1e-6
VMEM_BYTES = 24 * 2**20
F32 = jnp.float32
BF16 = jnp.bfloat16
NN = (((1,), (0,)), ((), ()))
NT = (((1,), (1,)), ((), ()))
TN = (((0,), (0,)), ((), ()))


def split(x):
    high = x.astype(BF16)
    low = (x - high.astype(F32)).astype(BF16)
    return high, low


def dot3(left, right, dims):
    def one(a, b):
        return lax.dot_general(a, b, dims, preferred_element_type=F32)

    return one(left[0], right[0]) + (one(left[0], right[1]) + one(left[1], right[0]))


def square3(parts):
    high, low = parts
    mixed = lax.dot_general(high, low, NN, preferred_element_type=F32)
    return lax.dot_general(high, high, NN, preferred_element_type=F32) + (mixed + jnp.transpose(mixed))


def call(kernel, name, out_shape, flops, **kwargs):
    return pl.pallas_call(
        kernel,
        out_shape=out_shape,
        compiler_params=pltpu.CompilerParams(vmem_limit_bytes=VMEM_BYTES),
        cost_estimate=pl.CostEstimate(flops=flops, bytes_accessed=2**22, transcendentals=0),
        name=name,
        **kwargs,
    )


VMEM = pl.BlockSpec(memory_space=pltpu.VMEM)
HBM = pl.BlockSpec(memory_space=pltpu.HBM)


def in_hbm(x):
    return pltpu.with_memory_space_constraint(x, pltpu.HBM)


def in_vmem(x):
    return pltpu.with_memory_space_constraint(x, pltpu.VMEM)


def row_tiles(ref, tile):
    return [pl.ds(start, tile) for start in range(0, ref.shape[0], tile)]


def outer3(e, o, dims):
    def one(a, b, dims):
        return lax.dot_general(a, b, dims, preferred_element_type=F32)

    mixed = one(e[0], e[1], NN) + one(o[0], o[1], dims)
    return (one(e[0], e[0], NN) + one(o[0], o[0], dims)) + (mixed + jnp.transpose(mixed))


def two_steps(e1, e2, o, eye):
    op, e1p, e2p = split(o), split(e1), split(e2)
    d1 = eye - outer3(e1p, op, NT)
    d2 = eye - outer3(e2p, op, TN)
    w1, w2 = weights(d1, d2, eye)
    w1, w2 = split(w1), split(w2)
    o = dot3(w1, op, NN)
    return dot3(w1, e1p, NN), dot3(w2, e2p, NN), o


def weights(d1, d2, eye):
    d1p, d2p = split(d1), split(d2)
    q1 = square3(d1p)
    q2 = square3(d2p)
    i1 = split(0.375 * eye + 0.3125 * d1 + 0.0625 * q1)
    i2 = split(0.375 * eye + 0.3125 * d2 + 0.0625 * q2)
    w1 = eye + 0.5 * d1 + dot3(split(q1), i1, NN)
    w2 = eye + 0.5 * d2 + dot3(split(q2), i2, NN)
    return w1, w2


def rotation_kernel(index, movers_ref, packed_ref, *outs):
    left = [packed_ref[CHUNK * k:CHUNK * k + 8, :] for k in range(SLABS)]
    right = [packed_ref[CHUNK * k + 8:CHUNK * k + 16, :] for k in range(SLABS)]
    cross = jnp.concatenate([jnp.concatenate(left, 0), jnp.concatenate(right, 0)], 1)
    norms = packed_ref[16:20, :]
    for k in range(1, SLABS):
        norms = norms + packed_ref[CHUNK * k + 16:CHUNK * k + 20, :]
    norm_a = jnp.concatenate([norms[0:1], norms[1:2]], 1)
    norm_m = jnp.concatenate([norms[2:3], norms[3:4]], 1)
    rows = lax.broadcasted_iota(jnp.int32, (HALF, HALF), 0)
    cols = lax.broadcasted_iota(jnp.int32, (HALF, HALF), 1)
    eye = (rows == cols).astype(F32)
    norm_a = jnp.transpose(jnp.broadcast_to(norm_a, (8, HALF)))[:, :1]
    diff = norm_a - norm_m
    total = norm_a + norm_m
    skew = -cross * diff / (diff * diff + 0.25 * total * total + EPS)
    scale = 1.0 / (4.0 * jnp.sqrt(PAIR + 2.0 * jnp.sum(skew * skew, keepdims=True)))
    start = scale * skew
    parts = split(start)
    own = (1.0 - scale * scale) * eye
    w1, w2 = weights(own - dot3(parts, parts, NT), own - dot3(parts, parts, TN), eye)
    e1, e2, o = scale * w1, scale * w2, dot3(split(w1), parts, NN)
    for _ in range(5):
        e1, e2, o = two_steps(e1, e2, o, eye)
    minus_ot = -jnp.transpose(o)

    firsts = movers_ref[index] == 1

    def put(move_a, move_m, stay_a, stay_m):
        if len(outs) == 2:
            for i, block in enumerate((move_a, move_m, stay_a, stay_m)):
                outs[0][HALF * i:HALF * i + HALF, :] = block
        else:
            outs[0][...], outs[1][...] = move_a, move_m
        outs[-1][:HALF, :] = stay_a
        outs[-1][HALF:, :] = stay_m

    @pl.when(firsts)
    def _():
        put(e1, minus_ot, o, e2)

    @pl.when(jnp.logical_not(firsts))
    def _():
        put(o, e2, e1, minus_ot)


def rotation(index, movers, packed, sizes):
    return call(
        lambda *refs: rotation_kernel(index, *refs),
        "rotation",
        [jax.ShapeDtypeStruct((n, HALF), F32) for n in sizes],
        10**10,
        in_specs=[pl.BlockSpec(memory_space=pltpu.SMEM), VMEM],
        out_specs=[VMEM] * len(sizes),
    )(movers, packed)


def pack(packed_ref, value):
    width = value.shape[1]
    per = 8 * width // 128
    for k in range(SLABS):
        for b in range(width // 128):
            packed_ref[per * k + 8 * b:per * k + 8 * b + 8, :] = value[8 * k:8 * k + 8, 128 * b:128 * b + 128]


def squares(x):
    return jnp.sum(x.reshape(-1, 8, x.shape[1]) ** 2, axis=0)


def first_kernel(x_ref, packed_ref, norm_ref):
    total, norm = 0.0, 0.0
    for rows in row_tiles(x_ref, 256):
        x = x_ref[rows, :]
        total += dot3(split(x[:, :HALF]), split(x[:, HALF:]), TN)
        norm += squares(x)
    pack(packed_ref, total)
    norm_ref[...] = jnp.concatenate([norm[:, :HALF], norm[:, HALF:]], 0)


def first_inner(x):
    return call(
        first_kernel,
        "first_inner",
        (jax.ShapeDtypeStruct((HALF * HALF // 128, 128), F32), jax.ShapeDtypeStruct((16, HALF), F32)),
        6 * x.shape[0] * HALF * HALF,
        in_specs=[VMEM],
        out_specs=[VMEM] * 2,
    )(in_vmem(x))


def meet_kernel(x_ref, q_ref, left_ref, a_ref, norm_ref, packed_ref):
    q = split(q_ref[...])
    norm, total = 0.0, 0.0
    for rows in row_tiles(x_ref, 512):
        a = dot3(split(x_ref[rows, :]), q, NN)
        a_ref[rows, :] = a
        norm += squares(a)
    norm_ref[...] = norm
    for rows in row_tiles(x_ref, 512):
        total += dot3(split(a_ref[rows, :]), split(left_ref[rows, :]), TN)
    pack(packed_ref, total)


def meet(x, q, left):
    rows = x.shape[0]
    return call(
        meet_kernel,
        "meet",
        (
            jax.ShapeDtypeStruct((rows, HALF), F32),
            jax.ShapeDtypeStruct((8, HALF), F32),
            jax.ShapeDtypeStruct((HALF * PAIR // 128, 128), F32),
        ),
        12 * rows * PAIR * HALF,
        in_specs=[VMEM] * 3,
        out_specs=[VMEM] * 3,
    )(in_vmem(x), q, in_vmem(left))


def fill(out_ref, cross, norm_a, norm_m):
    norm_a = jnp.sum(norm_a, axis=0, keepdims=True)
    norm_m = jnp.sum(norm_m, axis=0, keepdims=True)
    chunk = jnp.concatenate(
        [cross[:, :128], cross[:, 128:], norm_a[:, :128], norm_a[:, 128:], norm_m[:, :128], norm_m[:, 128:]], 0
    )
    for k in range(SLABS):
        out_ref[CHUNK * k:CHUNK * k + CHUNK, :] = chunk


def share_kernel(parts_ref, norm_ref, out_ref):
    total = parts_ref[0:16, :]
    for k in range(1, SLABS):
        total = total + parts_ref[16 * k:16 * k + 16, :]
    cross = jnp.concatenate([total[:8], total[8:]], 1)
    fill(out_ref, cross, norm_ref[:8, :], norm_ref[8:, :])


def project_kernel(parts_ref, high_ref, low_ref, norm_a_ref, norm_m_ref, out_ref):
    total = parts_ref[0:32, :]
    for k in range(1, SLABS):
        total = total + parts_ref[32 * k:32 * k + 32, :]
    wide = jnp.concatenate([total[8 * b:8 * b + 8] for b in range(4)], 1)
    wide = jnp.concatenate([wide, wide], 0)
    cross = dot3(split(wide), (high_ref[...], low_ref[...]), NN)[:8]
    fill(out_ref, cross, norm_a_ref[...], norm_m_ref[...])


def payload(kernel, *arrays):
    out = jax.ShapeDtypeStruct((SLABS * CHUNK, 128), F32)
    return call(kernel, "payload", out, 10**7, in_specs=[VMEM] * len(arrays), out_specs=VMEM)(*arrays)


def turn_kernel(
    x_ref, q_ref, out_ref, norm_ref, high_ref, low_ref, a_high_ref, a_low_ref, held_ref, turn_ref, part_ref, sems
):
    pltpu.sync_copy(q_ref, turn_ref)
    move, stay = split(turn_ref[:PAIR, :]), split(turn_ref[PAIR:, :])
    high_ref[...], low_ref[...] = move
    norm, outs = 0.0, []
    for i, rows in enumerate(row_tiles(x_ref, 512)):
        x = split(x_ref[rows, :])
        out = dot3(x, move, NN)
        held_ref[rows, :] = out
        norm += squares(out)
        part_ref[0, rows, :], part_ref[1, rows, :] = split(dot3(x, stay, NN))
        goes = ((held_ref, out_ref), (part_ref.at[0], a_high_ref), (part_ref.at[1], a_low_ref))
        for j, (here, there) in enumerate(goes):
            outs.append(pltpu.make_async_copy(here.at[rows], there.at[rows], sems.at[i, j]))
            outs[-1].start()
    norm_ref[...] = norm
    for copy in outs:
        copy.wait()


def turn(x, q):
    rows = x.shape[0]
    part = pltpu.HBM((rows, HALF), BF16)
    return call(
        turn_kernel,
        "turn",
        (
            pltpu.HBM((rows, HALF), F32),
            jax.ShapeDtypeStruct((8, HALF), F32),
            jax.ShapeDtypeStruct((PAIR, HALF), BF16),
            jax.ShapeDtypeStruct((PAIR, HALF), BF16),
            part,
            part,
        ),
        30 * 10**9,
        in_specs=[VMEM, HBM],
        out_specs=[HBM] + [VMEM] * 3 + [HBM] * 2,
        scratch_shapes=[
            pltpu.VMEM((rows, HALF), F32),
            pltpu.VMEM((2 * PAIR, HALF), F32),
            pltpu.VMEM((2, rows, HALF), BF16),
            pltpu.SemaphoreType.DMA((rows // 512, 3)),
        ],
    )(in_vmem(x), in_hbm(q))


def ready_kernel(m_ref, high_ref, low_ref):
    high_ref[...], low_ref[...] = split(m_ref[...])


def ready(m):
    out = jax.ShapeDtypeStruct(m.shape, BF16)
    return call(
        ready_kernel,
        "ready",
        (out, out),
        10**6,
        in_specs=[VMEM],
        out_specs=[VMEM] * 2,
    )(in_vmem(m))


def right_a_kernel(high_ref, low_ref, q_ref, out_ref):
    q = split(q_ref[...])
    for rows in row_tiles(high_ref, 512):
        out_ref[rows, :] = dot3((high_ref[rows, :], low_ref[rows, :]), q, NN)


def right_a(high, low, q):
    rows = high.shape[0]
    return call(
        right_a_kernel,
        "right_a",
        jax.ShapeDtypeStruct((rows, HALF), F32),
        6 * rows * HALF * HALF,
        in_specs=[VMEM] * 3,
        out_specs=VMEM,
    )(high, low, q)


def right_kernel(high_ref, low_ref, q_ref, part_ref, onto_ref, out_ref, held_ref, sems):
    q = split(q_ref[...])
    outs = []
    for i, rows in enumerate(row_tiles(high_ref, 256)):
        held_ref[rows, :] = part_ref[rows, :] + dot3((high_ref[rows, :], low_ref[rows, :]), q, NN)
        outs.append(pltpu.make_async_copy(held_ref.at[rows], out_ref.at[rows, pl.ds(HALF, HALF)], sems.at[i]))
        outs[-1].start()
    for copy in outs:
        copy.wait()


def right(high, low, q, part, onto):
    rows = high.shape[0]
    return call(
        right_kernel,
        "right",
        jax.ShapeDtypeStruct((rows, PAIR), F32),
        6 * rows * HALF * HALF,
        in_specs=[VMEM] * 4 + [HBM],
        out_specs=HBM,
        scratch_shapes=[pltpu.VMEM((rows, HALF), F32), pltpu.SemaphoreType.DMA((rows // 256,))],
        input_output_aliases={4: 0},
    )(high, low, q, part, onto)


def left_kernel(a_ref, m_ref, q_ref, out_ref, held_ref, sems):
    qa, qm = split(q_ref[:HALF, :]), split(q_ref[HALF:, :])
    outs = []
    for i, rows in enumerate(row_tiles(a_ref, 512)):
        held_ref[rows, :] = dot3(split(a_ref[rows, :]), qa, NN) + dot3(split(m_ref[rows, :]), qm, NN)
        outs.append(pltpu.make_async_copy(held_ref.at[rows], out_ref.at[rows, pl.ds(0, HALF)], sems.at[i]))
        outs[-1].start()
    for copy in outs:
        copy.wait()


def left(a, m, q):
    rows = a.shape[0]
    return call(
        left_kernel,
        "left",
        jax.ShapeDtypeStruct((rows, PAIR), F32),
        6 * rows * PAIR * HALF,
        in_specs=[VMEM] * 3,
        out_specs=HBM,
        scratch_shapes=[pltpu.VMEM((rows, HALF), F32), pltpu.SemaphoreType.DMA((rows // 512,))],
    )(a, in_vmem(m), q)


def passed_along(value):
    count = lax.axis_size("blk")
    return lax.ppermute(value, "blk", [(source, (source + 1) % count) for source in range(count)])


def exchanged(packed, shape):
    return lax.all_to_all(packed.reshape(SLABS, *shape), "slab", 0, 0).reshape(packed.shape)


def local(columns, movers):
    left_columns = passed_along(columns)

    cross, norms = first_inner(columns)
    movers, cross = lax.optimization_barrier((movers[:, 0], cross))
    parts = exchanged(cross, (16, 128))
    packed = exchanged(payload(share_kernel, parts, norms), (CHUNK // 2, 2, 128))
    both, stay = rotation(0, movers, packed, (2 * PAIR, PAIR))

    left_both = passed_along(both)
    a, norm_a, cross = meet(columns, stay, left_columns)
    parts = exchanged(cross, (32, 128))
    m, norm_m, high, low, *left_a = turn(left_columns, left_both)
    left_m = passed_along(m)
    packed = exchanged(payload(project_kernel, parts, high, low, norm_a, norm_m), (CHUNK // 2, 2, 128))
    move_a, move_m, stay = rotation(1, movers, packed, (HALF, HALF, PAIR))

    left_move_a = passed_along(move_a)
    left_move_m = passed_along(move_m)
    left_m = ready(left_m)
    out = left(a, m, stay)
    left_a, left_m, out = lax.optimization_barrier((left_a, left_m, out))
    part = right_a(*left_a, left_move_a)
    return right(*left_m, left_move_m, part, out)


def solution(mesh):
    placed = (P("slab", "blk"), P(None, "blk"))
    return jax.shard_map(
        local, mesh=mesh, in_specs=placed, out_specs=P("slab", "blk"), check_vma=False
    )
```
